256 devices in a mesh: section: 64 (over z, y, core), rep: 4 (over x).
Axes of the slice: x: 4, y: 4, z: 8, core: 2. Of those that a mesh axis runs over, the one named last changes fastest.
Arguments:
- document_token_embedding: bfloat16 [8, 128, 4096], P('rep'), may hold values from -6 to 6
- doc_lengths: int32 [8, 4], P('rep'), may hold values from 1 to 32, as said below
- docid_embed: bfloat16 [8, 32, 4096], P('rep'), may hold values from -6 to 6
- docid_targets: int32 [8, 32], P('rep'), may hold values from 0 to 16383
- enc_gain: float32 [5, 4096], replicated, may hold values from 0.1 to 1.9
- dec_gain: float32 [2, 4096], replicated, may hold values from 0.1 to 1.9
- w_enc_qkv: bfloat16 [3, 12288, 4096], P(None, 'section'), may hold values from -0.03125 to 0.03125
- w_enc_out: bfloat16 [12288, 4096], P('section'), may hold values from -0.75 to 0.75
- cross_query_key_value_weight: bfloat16 [3, 4096, 4096], P(None, 'section'), may hold values from -0.03125 to 0.03125
- w_cross_out: bfloat16 [4096, 4096], P('section'), may hold values from -0.75 to 0.75
- docid_head_weight: bfloat16 [4096, 16384], P(None, 'section'), may hold values from -0.25 to 0.25
Outputs:
- logits: bfloat16 [8, 32, 16384], P('rep', None, 'section')
- token_loss: float32 [8, 32], P('rep')
- mean_loss: float32 [], replicated
The draws below stay inside these ranges and needn't reach their ends.
Inputs may be any that keep to these rules, and one draw needn't show every extreme that they name: `doc_lengths`: in every draw some document has exactly 32 tokens.
All inputs are finite; a program needn't handle non-finite values.
Results may differ from the reference program's by a relative error of at most 0.019.
Values may be sent and summed in bfloat16 or wider, within the bound.
No kernel may reach another device: no remote copies, remote signals or barrier semaphores. Data moves between devices by JAX's collectives and lax.ppermute only.
A program may use at most 64 MiB of HBM per device.

```python
import jax
import jax.numpy as jnp
from jax import lax

D = 4096
HD = 64
XHEADS = 64
HEADS = 48
VOCAB = 16384
GROUPS = 4
DOCS = 4
DLEN = 8
LMAX = 32
ROWS = 128
DROWS = 32
BATCH = 8


def draw_doc_lengths(key, part):
    key_left, key_right, key_pick = jax.random.split(jax.random.fold_in(key, 17), 3)
    left_draw = jax.random.randint(key_left, (BATCH, DOCS), 0, LMAX)
    right_draw = jax.random.randint(key_right, (BATCH, DOCS), 0, LMAX)
    lengths = 1 + left_draw * right_draw // LMAX
    chosen = jax.random.randint(key_pick, (), 0, BATCH * DOCS)
    flattened = jnp.where(jnp.arange(BATCH * DOCS) == chosen, LMAX, lengths.reshape(-1))
    return flattened.reshape(BATCH, DOCS).astype(jnp.int32)


def touch_ends(array, stream_key, low, top_value):
    extent = array.shape
    place = [jax.random.randint(jax.random.fold_in(stream_key, axis), (), 0, extent[axis]) for axis in range(len(extent))]
    array = array.at[tuple(place)].set(low)
    longest = extent.index(max(extent))
    place[longest] = (place[longest] + 1) % extent[longest]
    return array.at[tuple(place)].set(top_value)


def block_levels(rng, shape, shards, low, top_value):
    def one(dim, shards_of):
        steps = jax.random.uniform(jax.random.fold_in(jax.random.fold_in(rng, 6), dim), (shards_of,), jnp.float32, low / len(shards), top_value / len(shards))
        return jnp.repeat(jnp.exp(steps), shape[dim] // shards_of).reshape((-1,) + (1,) * (len(shape) - dim - 1))

    level = one(*shards[0])
    for cut in shards[1:]:
        level = level * one(*cut)
    return level


def noise(own_key, extent, spread, reach, pieces=(), dtype=jnp.bfloat16):
    array = jax.random.normal(own_key, extent, jnp.float32) * spread
    if len(pieces) > 0:
        array = block_levels(own_key, extent, pieces, -0.22, 0.18) * array
    return jnp.clip(array, min=-reach, max=reach).astype(dtype)


def setup_inputs(seed: int = 0) -> dict:
    seeds = jax.random.split(jax.random.key(seed), 12)
    document_token_embedding = noise(seeds[0], (BATCH, ROWS, D), 1.0, 6.0, ((0, 4),))
    doc_lengths = draw_doc_lengths(jax.random.fold_in(seeds[11], 71), 0)
    docid_embed = noise(seeds[2], (BATCH, DROWS, D), 1.0, 6.0, ((0, 4),))
    docid_targets = touch_ends(jax.random.randint(seeds[3], (BATCH, DROWS), 0, VOCAB), jax.random.fold_in(seeds[3], 1), 0, VOCAB - 1).astype(jnp.int32)
    enc_gain = jnp.clip(1.0 + 0.18 * jax.random.normal(seeds[4], (GROUPS + 1, D), jnp.float32), 0.1, 1.9)
    dec_gain = jnp.clip(1.0 + 0.18 * jax.random.normal(seeds[5], (2, D), jnp.float32), 0.1, 1.9)
    w_enc_qkv = noise(seeds[6], (3, GROUPS * HEADS * HD, D), (D * 8) ** -0.5, 0.03125, ((1, 64),))
    w_enc_out = noise(seeds[7], (GROUPS * HEADS * HD, D), HD ** -0.5, 0.75, ((0, 64),))
    cross_query_key_value_weight = noise(seeds[8], (3, XHEADS * HD, D), (D * 8) ** -0.5, 0.03125, ((1, 64),))
    w_cross_out = noise(seeds[9], (XHEADS * HD, D), HD ** -0.5, 0.75, ((0, 64),))
    docid_head_weight = noise(seeds[10], (D, VOCAB), (D // 9) ** -0.5, 0.25, ((1, 64),))
    return {"document_token_embedding": document_token_embedding, "doc_lengths": doc_lengths, "docid_embed": docid_embed, "docid_targets": docid_targets, "enc_gain": enc_gain, "dec_gain": dec_gain, "w_enc_qkv": w_enc_qkv, "w_enc_out": w_enc_out, "cross_query_key_value_weight": cross_query_key_value_weight, "w_cross_out": w_cross_out, "docid_head_weight": docid_head_weight}


def norm_rows(values, gain):
    values = values.astype(jnp.float32)
    scale = lax.rsqrt(lax.optimization_barrier(jnp.mean(values * values, axis=-1, keepdims=True)) + 1e-06)
    return values * scale * gain

def attend(queries, key_rows, values, allowed):
    scores = jnp.einsum('qhe,khe->hqk', queries.astype(jnp.float32), key_rows.astype(jnp.float32))
    attention_weight_rows = jnp.where(allowed[None], jnp.exp(scores), 0.0)
    probabilities = (attention_weight_rows / lax.optimization_barrier(jnp.sum(attention_weight_rows, axis=-1, keepdims=True))).astype(jnp.bfloat16)
    mixture = jnp.einsum('hqk,khe->qhe', probabilities.astype(jnp.float32), values.astype(jnp.float32))
    return mixture.astype(jnp.bfloat16)

def project(normed, weight):
    return jnp.dot(normed, weight.T, preferred_element_type=jnp.float32).astype(jnp.bfloat16)

def reference(document_token_embedding, doc_lengths, docid_embed, docid_targets, enc_gain, dec_gain, w_enc_qkv, w_enc_out, cross_query_key_value_weight, w_cross_out, docid_head_weight):
    width_heads = HEADS * HD
    positions = jnp.arange(DOCS * LMAX)
    key_doc = positions // LMAX
    key_place = positions % LMAX
    decoder_doc = jnp.arange(DOCS * DLEN) // DLEN

    def per_sample(sample):
        doc_rows, lengths, docid_rows, targets = sample
        live_keys = key_place < lengths[key_doc]
        allowed = (key_doc[:, None] == key_doc[None, :]) & live_keys[None, :]
        hidden = doc_rows
        for depth in range(GROUPS):
            normed = norm_rows(hidden, enc_gain[depth]).astype(jnp.bfloat16)
            lower = depth * width_heads
            upper = lower + width_heads
            projected = [project(normed, w_enc_qkv[member, lower:upper]).reshape(-1, HEADS, HD) for member in range(3)]
            mixture = attend(projected[0], projected[1], projected[2], allowed).reshape(-1, width_heads)
            update = jnp.dot(mixture, w_enc_out[lower:upper], preferred_element_type=jnp.float32)
            hidden = (hidden.astype(jnp.float32) + update).astype(jnp.bfloat16)
        encoder_memory = norm_rows(hidden, enc_gain[GROUPS]).astype(jnp.bfloat16)
        dec_normed = norm_rows(docid_rows, dec_gain[0]).astype(jnp.bfloat16)
        queries = project(dec_normed, cross_query_key_value_weight[0]).reshape(-1, XHEADS, HD)
        key_rows = project(encoder_memory, cross_query_key_value_weight[1]).reshape(-1, XHEADS, HD)
        values = project(encoder_memory, cross_query_key_value_weight[2]).reshape(-1, XHEADS, HD)
        cross_allowed = (decoder_doc[:, None] == key_doc[None, :]) & live_keys[None, :]
        mixture = attend(queries, key_rows, values, cross_allowed).reshape(-1, XHEADS * HD)
        update = jnp.dot(mixture, w_cross_out, preferred_element_type=jnp.float32)
        closing_rows = norm_rows(docid_rows.astype(jnp.float32) + update, dec_gain[1]).astype(jnp.bfloat16)
        scores_vocab = jnp.dot(closing_rows, docid_head_weight, preferred_element_type=jnp.float32)
        totals = jnp.log(lax.optimization_barrier(jnp.sum(jnp.exp(scores_vocab), axis=-1)))
        picked = jnp.take_along_axis(scores_vocab, targets[:, None].astype(jnp.int32), axis=-1)[:, 0]
        return (scores_vocab.astype(jnp.bfloat16), totals - picked)
    logits, token_loss = lax.map(per_sample, (document_token_embedding, doc_lengths, docid_embed, docid_targets))
    return (logits, token_loss, jnp.mean(token_loss))
```

```python
import jax
import jax.numpy as jnp
from jax import lax
from jax.sharding import PartitionSpec as P

HD = 64
GROUPS = 4
LANES_Y = 4
CHAINS = 2


def routed(block, pairs):
    return lax.ppermute(block, "section", pairs)


def lanes_of(group):
    return range(group * 16, group * 16 + 16)


def swapped(block, group, mask):
    return routed(block, [(s, s ^ mask) for s in lanes_of(group)])


CORE, ROW, PLANE = 1, 2, 8


def norm_rows(values, gain):
    values = values.astype(jnp.float32)
    scale = lax.rsqrt(jnp.mean(values * values, axis=-1, keepdims=True) + 1e-06)
    return values * scale * gain


def attend(queries, key_rows, values, allowed):
    scores = jnp.einsum("qhe,khe->hqk", queries, key_rows, preferred_element_type=jnp.float32)
    weights = jnp.where(allowed[None], jnp.exp(scores), 0.0)
    probabilities = (weights / jnp.sum(weights, axis=-1, keepdims=True)).astype(jnp.bfloat16)
    mixture = jnp.einsum("hqk,khe->qhe", probabilities, values, preferred_element_type=jnp.float32)
    return mixture.astype(jnp.bfloat16)


def gather_rows(own, group):
    pair = jnp.concatenate([own, swapped(own, group, PLANE)], 0)
    ring = jnp.concatenate(
        [pair] + [swapped(pair, group, ROW * k) for k in range(1, LANES_Y)], 0
    )
    return jnp.concatenate([ring, swapped(ring, group, CORE)], 0)


def reduce_rows(mixture, weight, group):
    half = mixture.shape[0] // 2
    away = jnp.dot(mixture[half:], weight, preferred_element_type=jnp.float32)
    arrived = swapped(away.astype(jnp.bfloat16), group, CORE)
    own = jnp.dot(mixture[:half], weight, preferred_element_type=jnp.float32)
    ring = own + arrived.astype(jnp.float32)
    quarter = half // LANES_Y
    sent = ring.astype(jnp.bfloat16)
    pair = ring[:quarter]
    for k in range(1, LANES_Y):
        block = swapped(sent[k * quarter : (k + 1) * quarter], group, ROW * k)
        pair = pair + block.astype(jnp.float32)
    eighth = quarter // 2
    arrived = swapped(pair[eighth:].astype(jnp.bfloat16), group, PLANE)
    return pair[:eighth] + arrived.astype(jnp.float32)


def shards(
    document_token_embedding,
    doc_lengths,
    docid_embed,
    docid_targets,
    enc_gain,
    dec_gain,
    w_enc_qkv,
    w_enc_out,
    cross_query_key_value_weight,
    w_cross_out,
    docid_head_weight,
):
    section_index = lax.axis_index("section")
    core = section_index % 2
    ring_y = section_index // 2 % LANES_Y
    plane = section_index // 8 % 2
    micro_count, row_count, model_width = document_token_embedding.shape
    doc_count = doc_lengths.shape[1]
    doc_span = row_count // doc_count
    decoder_rows = docid_embed.shape[1]
    docid_span = decoder_rows // doc_count
    local_heads = w_enc_qkv.shape[1] // HD
    lanes = 16
    last = GROUPS - 1

    def order_of(span):
        rows = span // 4
        index = jnp.arange(doc_count * span)
        kc = index // (doc_count * span // 2)
        ky = index // (2 * rows) % LANES_Y
        kz = index // rows % 2
        doc = ring_y ^ ky
        place = ((plane ^ kz) * 2 + (core ^ kc)) * rows + index % rows
        return doc, place

    enc_doc, enc_place = order_of(doc_span)
    dec_doc, dec_place = order_of(docid_span)
    enc_order = enc_doc * doc_span + enc_place
    dec_order = dec_doc * docid_span + dec_place
    same_doc = enc_doc[:, None] == enc_doc[None, :]
    cross_doc = dec_doc[:, None] == enc_doc[None, :]

    lengths_there = [jnp.take(doc_lengths[m], enc_doc) for m in range(micro_count)]
    live = [enc_place < lengths_there[m] for m in range(micro_count)]
    allowed = [same_doc & live[m][None, :] for m in range(micro_count)]
    cross_allowed = [cross_doc & live[m][None, :] for m in range(micro_count)]

    docid_rows = jnp.take(docid_embed, dec_order, axis=1)
    dec_normed = norm_rows(docid_rows, dec_gain[0]).astype(jnp.bfloat16)
    own_queries = jnp.einsum(
        "brd,cd->brc",
        dec_normed,
        cross_query_key_value_weight[0],
        preferred_element_type=jnp.float32,
    ).astype(jnp.bfloat16)

    def to_last(block):
        pieces = [block]
        for k in range(1, GROUPS):
            pairs = [(s - k * lanes, s) for s in lanes_of(last)]
            pieces.append(routed(block, pairs))
        return pieces

    cross_queries = jnp.stack(to_last(own_queries), 2)
    cross_maps = jnp.concatenate(to_last(cross_query_key_value_weight[1:]), 1)
    cross_out = jnp.concatenate(to_last(w_cross_out), 0)

    def project(normed):
        return jnp.einsum(
            "rd,mcd->mrc", normed, w_enc_qkv, preferred_element_type=jnp.float32
        ).astype(jnp.bfloat16)

    def mix(normed, mask):
        projected = project(normed).reshape(3, row_count, local_heads, HD)
        return attend(projected[0], projected[1], projected[2], mask).reshape(row_count, -1)

    block_rows = row_count // lanes
    hidden = []
    for m in range(micro_count):
        rows = jnp.take(document_token_embedding[m], enc_order, axis=0)
        normed = norm_rows(rows, enc_gain[0]).astype(jnp.bfloat16)
        summed = reduce_rows(mix(normed, allowed[m]), w_enc_out, 0)
        hidden.append((rows[:block_rows].astype(jnp.float32) + summed).astype(jnp.bfloat16))
    for group in range(1, GROUPS):
        for m in range(micro_count):
            own = routed(hidden[m], [(s - lanes, s) for s in lanes_of(group)])
            normed = gather_rows(norm_rows(own, enc_gain[group]).astype(jnp.bfloat16), group)
            summed = reduce_rows(mix(normed, allowed[m]), w_enc_out, group)
            hidden[m] = (own.astype(jnp.float32) + summed).astype(jnp.bfloat16)

    mixtures = []
    for m in range(micro_count):
        memory = gather_rows(norm_rows(hidden[m], enc_gain[GROUPS]).astype(jnp.bfloat16), last)
        heads = jnp.einsum(
            "rd,qcd->qrc", memory, cross_maps, preferred_element_type=jnp.float32
        ).astype(jnp.bfloat16)
        heads = heads.reshape(2, row_count, GROUPS, HD)
        mixtures.append(
            attend(cross_queries[m], heads[0], heads[1], cross_allowed[m]).reshape(
                decoder_rows, -1
            )
        )
    share = docid_span // 4

    def interleaved(pieces):
        stacked = jnp.stack([p.reshape(lanes, share, -1) for p in pieces], 1)
        return stacked.reshape(lanes * micro_count * share, -1)

    own_docid = jnp.concatenate([docid_rows[m, :share] for m in range(micro_count)], 0)
    cross_sum = reduce_rows(interleaved(mixtures), cross_out, last)
    final_own = norm_rows(own_docid.astype(jnp.float32) + cross_sum, dec_gain[1]).astype(
        jnp.bfloat16
    )
    other = swapped(final_own, last, PLANE)
    first_half = jnp.where(plane == 0, final_own, other)
    second_half = jnp.where(plane == 0, other, final_own)
    final_pair = jnp.concatenate([first_half, second_half], 0)
    depth = section_index // 8
    for step, (up, down) in enumerate((((7, 0), (6, 5)), ((0, 1), (5, 4)), ((1, 2), (4, 3)))):
        pairs = [(up[0] * 8 + s, up[1] * 8 + s) for s in range(8)]
        pairs += [(down[0] * 8 + s, down[1] * 8 + s) for s in range(8)]
        arrived = routed(final_pair, pairs)
        final_pair = jnp.where((depth == up[1]) | (depth == down[1]), arrived, final_pair)
    everyone = range(64)
    ring = jnp.concatenate(
        [final_pair]
        + [
            routed(final_pair, [(s, s ^ (ROW * k)) for s in everyone]) for k in range(1, LANES_Y)
        ],
        0,
    )
    closing = jnp.concatenate([ring, routed(ring, [(s, s ^ CORE) for s in everyone])], 0)

    scores_here = jnp.dot(closing, docid_head_weight, preferred_element_type=jnp.float32)
    vocab_local = docid_head_weight.shape[1]
    index = jnp.arange(micro_count * decoder_rows)
    micro = index // decoder_rows
    doc = index // docid_span % doc_count
    place = index % docid_span
    half, quarter, row = place // (2 * share), place // share % 2, place % share
    source = ((((quarter ^ core) * LANES_Y + (doc ^ ring_y)) * 2 + half) * micro_count + micro)
    scores_vocab = jnp.take(scores_here, source * share + row, axis=0).reshape(
        micro_count, decoder_rows, vocab_local
    )
    vocab_start = section_index * vocab_local
    matches = docid_targets[..., None] == vocab_start + jnp.arange(vocab_local)
    parts = jnp.stack(
        [
            jnp.sum(jnp.exp(scores_vocab), axis=-1),
            jnp.sum(jnp.where(matches, scores_vocab, 0.0), axis=-1),
        ]
    ).reshape(1, -1)
    size = lax.axis_size("section")
    everything = lax.all_to_all(
        jnp.broadcast_to(parts[None], (size, *parts.shape)), "section", 0, 0, tiled=True
    )
    exponent_total, picked = jnp.sum(everything, axis=0).reshape(
        2, micro_count, decoder_rows
    )
    token_loss = jnp.log(exponent_total) - picked
    total = jnp.sum(token_loss).reshape(1, 1)
    for mask in (1, 3):
        total = total + lax.ppermute(total, "rep", [(i, i ^ mask) for i in range(4)])
    mean_loss = total[0, 0] / (token_loss.size * lax.axis_size("rep"))
    return (scores_vocab.astype(jnp.bfloat16), token_loss, mean_loss)


def solution(mesh):
    in_specs = (
        P("rep", None, None),
        P("rep", None),
        P("rep", None, None),
        P("rep", None),
        P(),
        P(),
        P(None, "section", None),
        P("section", None),
        P(None, "section", None),
        P("section", None),
        P(None, "section"),
    )
    out_specs = (P("rep", None, "section"), P("rep", None), P())
    return jax.shard_map(shards, mesh=mesh, in_specs=in_specs, out_specs=out_specs, check_vma=False)
```

```python
import jax
import jax.numpy as jnp
from jax import lax
from jax.sharding import PartitionSpec as P

HD = 64
GROUPS = 4


CORE, PLANE, GROUP = 1, 8, 16
RING = (2, 4, 6)
SIZE = 64


def exchanged(block, mask):
    return lax.ppermute(block, "section", [(s, s ^ mask) for s in range(SIZE)])


def norm_rows(values, gain):
    values = values.astype(jnp.float32)
    scale = lax.rsqrt(jnp.mean(values * values, axis=-1, keepdims=True) + 1e-06)
    return values * scale * gain


def attend(queries, key_rows, values, allowed):
    scores = jnp.einsum("qhe,khe->hqk", queries, key_rows, preferred_element_type=jnp.float32)
    weights = jnp.where(allowed[None], jnp.exp(scores), 0.0)
    probabilities = (weights / jnp.sum(weights, axis=-1, keepdims=True)).astype(jnp.bfloat16)
    mixture = jnp.einsum("hqk,khe->qhe", probabilities, values, preferred_element_type=jnp.float32)
    return mixture.astype(jnp.bfloat16)


def gather_rows(own):
    ring = jnp.concatenate([own] + [exchanged(own, mask) for mask in RING], 0)
    return jnp.concatenate([ring, exchanged(ring, CORE)], 0)


def reduce_rows(mixture, weight):
    half = mixture.shape[0] // 2
    away = jnp.dot(mixture[half:], weight, preferred_element_type=jnp.float32)
    arrived = exchanged(away.astype(jnp.bfloat16), CORE)
    own = jnp.dot(mixture[:half], weight, preferred_element_type=jnp.float32)
    ring = own + arrived.astype(jnp.float32)
    rows = half // 4
    sent = ring.astype(jnp.bfloat16)
    total = ring[:rows]
    for k, mask in enumerate(RING):
        block = exchanged(sent[(k + 1) * rows : (k + 2) * rows], mask)
        total = total + block.astype(jnp.float32)
    mine = total.astype(jnp.bfloat16)
    return mine.astype(jnp.float32) + exchanged(mine, PLANE).astype(jnp.float32)


def shards(
    document_token_embedding,
    doc_lengths,
    docid_embed,
    docid_targets,
    enc_gain,
    dec_gain,
    w_enc_qkv,
    w_enc_out,
    cross_query_key_value_weight,
    w_cross_out,
    docid_head_weight,
):
    section_index = lax.axis_index("section")
    core = section_index % 2
    ring_y = section_index // 2 % 4
    depth = section_index // PLANE
    group_index = section_index // GROUP
    micro_count, row_count, model_width = document_token_embedding.shape
    doc_count = doc_lengths.shape[1]
    doc_span = row_count // doc_count
    decoder_rows = docid_embed.shape[1]
    docid_span = decoder_rows // doc_count
    local_heads = w_enc_qkv.shape[1] // HD
    block_rows = doc_span // 2
    share = docid_span // 2

    index = jnp.arange(row_count)
    doc_there = ring_y ^ (index // block_rows % doc_count)
    place_there = (core ^ (index // (row_count // 2))) * block_rows + index % block_rows
    doc_plain, place_plain = index // doc_span, index % doc_span
    same_there = doc_there[:, None] == doc_there[None, :]
    same_plain = doc_plain[:, None] == doc_plain[None, :]

    def mix(normed, same, doc, place, lengths):
        live = place < jnp.sum(
            jnp.where(doc[:, None] == jnp.arange(doc_count), lengths[None, :], 0), axis=1
        )
        projected = jnp.einsum(
            "rd,mcd->mrc", normed, w_enc_qkv, preferred_element_type=jnp.float32
        ).astype(jnp.bfloat16)
        projected = projected.reshape(3, row_count, local_heads, HD)
        allowed = same & live[None, :]
        return attend(projected[0], projected[1], projected[2], allowed).reshape(row_count, -1)

    own_start = ring_y * doc_span + core * block_rows

    def own_of(m):
        return lax.dynamic_slice_in_dim(document_token_embedding[m], own_start, block_rows, 0)

    layer_gain = lax.dynamic_index_in_dim(enc_gain, group_index, 0, keepdims=False)
    normed = norm_rows(document_token_embedding[0], enc_gain[0]).astype(jnp.bfloat16)
    mixture = mix(normed, same_plain, doc_plain, place_plain, doc_lengths[0])
    mixture = jnp.take(mixture, doc_there * doc_span + place_there, axis=0)
    current = own_of(0)
    results = []
    for step in range(micro_count + GROUPS - 1):
        if step:
            slot = jnp.clip(step - group_index, 0, micro_count - 1)
            lengths = lax.dynamic_index_in_dim(doc_lengths, slot, 0, keepdims=False)
            handed = lax.ppermute(
                results[-1], "section", [(s - GROUP, s) for s in range(GROUP, SIZE)]
            )
            current = handed
            if step < micro_count:
                current = jnp.where(group_index == 0, own_of(step), handed)
            normed = gather_rows(norm_rows(current, layer_gain).astype(jnp.bfloat16))
            mixture = mix(normed, same_there, doc_there, place_there, lengths)
        summed = reduce_rows(mixture, w_enc_out)
        results.append((current.astype(jnp.float32) + summed).astype(jnp.bfloat16))

    def to_last(block):
        pieces = [block]
        for k in range(1, GROUPS):
            pairs = [(s - k * GROUP, s) for s in range(SIZE - GROUP, SIZE)]
            pieces.append(lax.ppermute(block, "section", pairs))
        return pieces

    index = jnp.arange(micro_count * decoder_rows)
    query_core = index // (micro_count * decoder_rows // 2)
    query_ring = index // (micro_count * share) % doc_count
    query_micro, query_row = index // share % micro_count, index % share
    query_doc = ring_y ^ query_ring
    query_order = (
        query_micro * decoder_rows
        + query_doc * docid_span
        + (core ^ query_core) * share
        + query_row
    )
    dec_normed = norm_rows(docid_embed, dec_gain[0]).astype(jnp.bfloat16)
    own_queries = jnp.dot(
        dec_normed.reshape(-1, model_width),
        cross_query_key_value_weight[0].T,
        preferred_element_type=jnp.float32,
    ).astype(jnp.bfloat16)
    cross_queries = jnp.stack(to_last(jnp.take(own_queries, query_order, axis=0)), 1)
    cross_maps = to_last(cross_query_key_value_weight[1:])
    cross_outs = to_last(w_cross_out)

    finished = jnp.concatenate(results[-micro_count:], 0)
    memory = gather_rows(norm_rows(finished, enc_gain[GROUPS]).astype(jnp.bfloat16))
    index = jnp.arange(micro_count * row_count)
    key_core = index // (micro_count * row_count // 2)
    key_doc = ring_y ^ (index // (micro_count * block_rows) % doc_count)
    key_micro = index // block_rows % micro_count
    key_place = (core ^ key_core) * block_rows + index % block_rows
    owner = key_micro * doc_count + key_doc
    key_live = key_place < jnp.sum(
        jnp.where(
            owner[:, None] == jnp.arange(micro_count * doc_count),
            doc_lengths.reshape(1, -1),
            0,
        ),
        axis=1,
    )
    cross_allowed = (query_micro * doc_count + query_doc)[:, None] == owner[None, :]
    cross_allowed = cross_allowed & key_live[None, :]
    heads = jnp.einsum(
        "rd,qcd->qrc",
        memory,
        jnp.concatenate(cross_maps, 1),
        preferred_element_type=jnp.float32,
    ).astype(jnp.bfloat16)
    heads = heads.reshape(2, micro_count * row_count, GROUPS, HD)
    cross_mixture = attend(cross_queries, heads[0], heads[1], cross_allowed)
    cross_sum = reduce_rows(
        cross_mixture.reshape(micro_count * decoder_rows, -1), jnp.concatenate(cross_outs, 0)
    )
    own_docid = lax.dynamic_slice_in_dim(
        docid_embed, ring_y * docid_span + core * share, share, 1
    ).reshape(micro_count * share, model_width)
    closing_own = norm_rows(own_docid.astype(jnp.float32) + cross_sum, dec_gain[1]).astype(
        jnp.bfloat16
    )
    for up, down in (((7, 0), (6, 5)), ((0, 1), (5, 4)), ((1, 2), (4, 3))):
        pairs = [(z * PLANE + s, to * PLANE + s) for z, to in (up, down) for s in range(PLANE)]
        arrived = lax.ppermute(closing_own, "section", pairs)
        closing_own = jnp.where((depth == up[1]) | (depth == down[1]), arrived, closing_own)
    closing = gather_rows(closing_own)

    scores_here = jnp.dot(closing, docid_head_weight, preferred_element_type=jnp.float32)
    vocab_local = docid_head_weight.shape[1]
    index = jnp.arange(micro_count * decoder_rows)
    micro, doc = index // decoder_rows, index // docid_span % doc_count
    half, row = index // share % 2, index % share
    source = (((half ^ core) * doc_count + (doc ^ ring_y)) * micro_count + micro) * share + row
    scores_vocab = jnp.take(scores_here, source, axis=0).reshape(
        micro_count, decoder_rows, vocab_local
    )
    vocab_start = section_index * vocab_local
    matches = docid_targets[..., None] == vocab_start + jnp.arange(vocab_local)
    sums = jnp.stack(
        [
            jnp.sum(jnp.exp(scores_vocab), axis=-1),
            jnp.sum(jnp.where(matches, scores_vocab, 0.0), axis=-1),
        ]
    ).reshape(1, -1)
    for mask in (CORE, 2, 6, PLANE, 2 * PLANE, 4 * PLANE):
        sums = sums + exchanged(sums, mask)
    exponent_total, picked = sums.reshape(2, micro_count, decoder_rows)
    token_loss = jnp.log(exponent_total) - picked
    total = jnp.sum(token_loss).reshape(1, 1)
    for mask in (1, 3):
        total = total + lax.ppermute(total, "rep", [(i, i ^ mask) for i in range(4)])
    mean_loss = total[0, 0] / (token_loss.size * lax.axis_size("rep"))
    return (scores_vocab.astype(jnp.bfloat16), token_loss, mean_loss)


def solution(mesh):
    in_specs = (
        P("rep", None, None),
        P("rep", None),
        P("rep", None, None),
        P("rep", None),
        P(),
        P(),
        P(None, "section", None),
        P("section", None),
        P(None, "section", None),
        P("section", None),
        P(None, "section"),
    )
    out_specs = (P("rep", None, "section"), P("rep", None), P())
    return jax.shard_map(shards, mesh=mesh, in_specs=in_specs, out_specs=out_specs, check_vma=False)
```

```python
import jax
import jax.numpy as jnp
from jax import lax
from jax.sharding import PartitionSpec as P

HD = 64
GROUPS = 4


CORE, PLANE, GROUP = 1, 8, 16
RING = (2, 4, 6)
SIZE = 64


def exchanged(block, mask):
    return lax.ppermute(block, "section", [(s, s ^ mask) for s in range(SIZE)])


def norm_rows(values, gain):
    values = values.astype(jnp.float32)
    scale = lax.rsqrt(jnp.mean(values * values, axis=-1, keepdims=True) + 1e-06)
    return values * scale * gain


def attend(queries, key_rows, values, allowed):
    scores = jnp.einsum("qhe,khe->hqk", queries, key_rows, preferred_element_type=jnp.float32)
    weights = jnp.where(allowed[None], jnp.exp(scores), 0.0)
    probabilities = (weights / jnp.sum(weights, axis=-1, keepdims=True)).astype(jnp.bfloat16)
    mixture = jnp.einsum("hqk,khe->qhe", probabilities, values, preferred_element_type=jnp.float32)
    return mixture.astype(jnp.bfloat16)


def gather_rows(own):
    ring = jnp.concatenate([own] + [exchanged(own, mask) for mask in RING], 0)
    return jnp.concatenate([ring, exchanged(ring, CORE)], 0)


def along_z(block, route):
    pairs = [(z * PLANE + s, to * PLANE + s) for z, to in route for s in range(PLANE)]
    return lax.ppermute(block, "section", pairs)


def reduce_ring(mixture, weight):
    half = mixture.shape[0] // 2
    away = jnp.dot(mixture[half:], weight, preferred_element_type=jnp.float32)
    arrived = exchanged(away.astype(jnp.bfloat16), CORE)
    own = jnp.dot(mixture[:half], weight, preferred_element_type=jnp.float32)
    ring = own + arrived.astype(jnp.float32)
    rows = half // 4
    sent = ring.astype(jnp.bfloat16)
    total = ring[:rows]
    for k, mask in enumerate(RING):
        block = exchanged(sent[(k + 1) * rows : (k + 2) * rows], mask)
        total = total + block.astype(jnp.float32)
    return total


def add_exchanged(total, exchange):
    return total + exchange(total.astype(jnp.bfloat16)).astype(jnp.float32)


def shards(
    document_token_embedding,
    doc_lengths,
    docid_embed,
    docid_targets,
    enc_gain,
    dec_gain,
    w_enc_qkv,
    w_enc_out,
    cross_query_key_value_weight,
    w_cross_out,
    docid_head_weight,
):
    section_index = lax.axis_index("section")
    core = section_index % 2
    ring_y = section_index // 2 % 4
    depth = section_index // PLANE
    group_index = section_index // GROUP
    micro_count, row_count, model_width = document_token_embedding.shape
    doc_count = doc_lengths.shape[1]
    doc_span = row_count // doc_count
    decoder_rows = docid_embed.shape[1]
    docid_span = decoder_rows // doc_count
    local_heads = w_enc_qkv.shape[1] // HD
    block_rows = doc_span // 2
    share = docid_span // 2

    index = jnp.arange(row_count)
    doc_there = ring_y ^ (index // block_rows % doc_count)
    place_there = (core ^ (index // (row_count // 2))) * block_rows + index % block_rows
    doc_plain, place_plain = index // doc_span, index % doc_span
    same_there = doc_there[:, None] == doc_there[None, :]
    same_plain = doc_plain[:, None] == doc_plain[None, :]

    def mix(normed, same, doc, place, lengths):
        live = place < jnp.sum(
            jnp.where(doc[:, None] == jnp.arange(doc_count), lengths[None, :], 0), axis=1
        )
        projected = jnp.einsum(
            "rd,mcd->mrc", normed, w_enc_qkv, preferred_element_type=jnp.float32
        ).astype(jnp.bfloat16)
        projected = projected.reshape(3, row_count, local_heads, HD)
        allowed = same & live[None, :]
        return attend(projected[0], projected[1], projected[2], allowed).reshape(row_count, -1)

    own_start = ring_y * doc_span + core * block_rows

    def own_of(m):
        return lax.dynamic_slice_in_dim(document_token_embedding[m], own_start, block_rows, 0)

    layer_gain = lax.dynamic_index_in_dim(enc_gain, group_index, 0, keepdims=False)
    normed = norm_rows(document_token_embedding[0], enc_gain[0]).astype(jnp.bfloat16)
    mixture = mix(normed, same_plain, doc_plain, place_plain, doc_lengths[0])
    mixture = jnp.take(mixture, doc_there * doc_span + place_there, axis=0)
    current = own_of(0)
    results = []
    for step in range(micro_count + GROUPS - 1):
        if step:
            slot = jnp.clip(step - group_index, 0, micro_count - 1)
            lengths = lax.dynamic_index_in_dim(doc_lengths, slot, 0, keepdims=False)
            handed = lax.ppermute(
                results[-1], "section", [(s - GROUP, s) for s in range(GROUP, SIZE)]
            )
            current = handed
            if step < micro_count:
                current = jnp.where(group_index == 0, own_of(step), handed)
            normed = gather_rows(norm_rows(current, layer_gain).astype(jnp.bfloat16))
            mixture = mix(normed, same_there, doc_there, place_there, lengths)
        summed = reduce_ring(mixture, w_enc_out)
        summed = add_exchanged(summed, lambda block: exchanged(block, PLANE))
        results.append((current.astype(jnp.float32) + summed).astype(jnp.bfloat16))

    index = jnp.arange(micro_count * decoder_rows)
    query_core = index // (micro_count * decoder_rows // 2)
    query_ring = index // (micro_count * share) % doc_count
    query_micro, query_row = index // share % micro_count, index % share
    query_doc = ring_y ^ query_ring
    query_order = (
        query_micro * decoder_rows
        + query_doc * docid_span
        + (core ^ query_core) * share
        + query_row
    )
    dec_normed = norm_rows(docid_embed, dec_gain[0]).astype(jnp.bfloat16)
    own_queries = jnp.dot(
        dec_normed.reshape(-1, model_width),
        cross_query_key_value_weight[0].T,
        preferred_element_type=jnp.float32,
    ).astype(jnp.bfloat16)
    cross_queries = jnp.take(own_queries, query_order, axis=0)[:, None, :]

    finished = jnp.concatenate(results[-micro_count:], 0)
    own_memory = norm_rows(finished, enc_gain[GROUPS]).astype(jnp.bfloat16)
    arrived = [along_z(own_memory, ((7, to), (6, 5 - to))) for to in range(3)]
    for to in range(3):
        own_memory = jnp.where((depth == to) | (depth == 5 - to), arrived[to], own_memory)
    memory = gather_rows(own_memory)
    index = jnp.arange(micro_count * row_count)
    key_core = index // (micro_count * row_count // 2)
    key_doc = ring_y ^ (index // (micro_count * block_rows) % doc_count)
    key_micro = index // block_rows % micro_count
    key_place = (core ^ key_core) * block_rows + index % block_rows
    owner = key_micro * doc_count + key_doc
    key_live = key_place < jnp.sum(
        jnp.where(
            owner[:, None] == jnp.arange(micro_count * doc_count),
            doc_lengths.reshape(1, -1),
            0,
        ),
        axis=1,
    )
    cross_allowed = (query_micro * doc_count + query_doc)[:, None] == owner[None, :]
    cross_allowed = cross_allowed & key_live[None, :]
    heads = jnp.einsum(
        "rd,qcd->qrc",
        memory,
        cross_query_key_value_weight[1:],
        preferred_element_type=jnp.float32,
    ).astype(jnp.bfloat16)
    heads = heads.reshape(2, micro_count * row_count, -1, HD)
    cross_mixture = attend(cross_queries, heads[0], heads[1], cross_allowed)
    cross_sum = reduce_ring(cross_mixture.reshape(micro_count * decoder_rows, -1), w_cross_out)
    for partner in ((1, 0, 3, 2, 5, 4, 7, 6), (7, 2, 1, 4, 3, 6, 5, 0), (3, 6, 5, 0, 7, 2, 1, 4)):
        route = tuple(enumerate(partner))
        cross_sum = add_exchanged(cross_sum, lambda block, route=route: along_z(block, route))
    own_docid = lax.dynamic_slice_in_dim(
        docid_embed, ring_y * docid_span + core * share, share, 1
    ).reshape(micro_count * share, model_width)
    closing_own = norm_rows(own_docid.astype(jnp.float32) + cross_sum, dec_gain[1]).astype(
        jnp.bfloat16
    )
    closing = gather_rows(closing_own)

    scores_here = jnp.dot(closing, docid_head_weight, preferred_element_type=jnp.float32)
    vocab_local = docid_head_weight.shape[1]
    index = jnp.arange(micro_count * decoder_rows)
    micro, doc = index // decoder_rows, index // docid_span % doc_count
    half, row = index // share % 2, index % share
    source = (((half ^ core) * doc_count + (doc ^ ring_y)) * micro_count + micro) * share + row
    scores_vocab = jnp.take(scores_here, source, axis=0).reshape(
        micro_count, decoder_rows, vocab_local
    )
    vocab_start = section_index * vocab_local
    matches = docid_targets[..., None] == vocab_start + jnp.arange(vocab_local)
    sums = jnp.stack(
        [
            jnp.sum(jnp.exp(scores_vocab), axis=-1),
            jnp.sum(jnp.where(matches, scores_vocab, 0.0), axis=-1),
        ]
    ).reshape(1, -1)
    size = lax.axis_size("section")
    everything = lax.all_to_all(
        jnp.broadcast_to(sums[None], (size, *sums.shape)), "section", 0, 0, tiled=True
    )
    sums = jnp.sum(everything, axis=0)
    exponent_total, picked = sums.reshape(2, micro_count, decoder_rows)
    token_loss = jnp.log(exponent_total) - picked
    total = jnp.sum(token_loss).reshape(1, 1)
    for mask in (1, 3):
        total = total + lax.ppermute(total, "rep", [(i, i ^ mask) for i in range(4)])
    mean_loss = total[0, 0] / (token_loss.size * lax.axis_size("rep"))
    return (scores_vocab.astype(jnp.bfloat16), token_loss, mean_loss)


def solution(mesh):
    in_specs = (
        P("rep", None, None),
        P("rep", None),
        P("rep", None, None),
        P("rep", None),
        P(),
        P(),
        P(None, "section", None),
        P("section", None),
        P(None, "section", None),
        P("section", None),
        P(None, "section"),
    )
    out_specs = (P("rep", None, "section"), P("rep", None), P())
    return jax.shard_map(shards, mesh=mesh, in_specs=in_specs, out_specs=out_specs, check_vma=False)
```

```python
import jax
import jax.numpy as jnp
from jax import lax
from jax.sharding import PartitionSpec as P

HD = 64
GROUPS = 4


CORE, PLANE, GROUP = 1, 8, 16
RING = (2, 4, 6)
SIZE = 64


def exchanged(block, mask):
    return lax.ppermute(block, "section", [(s, s ^ mask) for s in range(SIZE)])


def norm_rows(values, gain):
    values = values.astype(jnp.float32)
    scale = lax.rsqrt(jnp.mean(values * values, axis=-1, keepdims=True) + 1e-06)
    return values * scale * gain


def attend(queries, key_rows, values, allowed):
    scores = jnp.einsum("qhe,khe->hqk", queries, key_rows, preferred_element_type=jnp.float32)
    weights = jnp.where(allowed[None], jnp.exp(scores), 0.0)
    probabilities = (weights / jnp.sum(weights, axis=-1, keepdims=True)).astype(jnp.bfloat16)
    mixture = jnp.einsum("hqk,khe->qhe", probabilities, values, preferred_element_type=jnp.float32)
    return mixture.astype(jnp.bfloat16)


def gather_rows(own):
    ring = jnp.concatenate([own] + [exchanged(own, mask) for mask in RING], 0)
    return jnp.concatenate([ring, exchanged(ring, CORE)], 0)


def along_z(block, route):
    pairs = [(z * PLANE + s, to * PLANE + s) for z, to in route for s in range(PLANE)]
    return lax.ppermute(block, "section", pairs)


def reduce_ring(mixture, weight):
    half = mixture.shape[0] // 2
    away = jnp.dot(mixture[half:], weight, preferred_element_type=jnp.float32)
    arrived = exchanged(away.astype(jnp.bfloat16), CORE)
    own = jnp.dot(mixture[:half], weight, preferred_element_type=jnp.float32)
    ring = own + arrived.astype(jnp.float32)
    rows = half // 4
    sent = ring.astype(jnp.bfloat16)
    total = ring[:rows]
    for k, mask in enumerate(RING):
        block = exchanged(sent[(k + 1) * rows : (k + 2) * rows], mask)
        total = total + block.astype(jnp.float32)
    return total


def add_exchanged(total, exchange):
    return total + exchange(total.astype(jnp.bfloat16)).astype(jnp.float32)


def shards(
    document_token_embedding,
    doc_lengths,
    docid_embed,
    docid_targets,
    enc_gain,
    dec_gain,
    w_enc_qkv,
    w_enc_out,
    cross_query_key_value_weight,
    w_cross_out,
    docid_head_weight,
):
    section_index = lax.axis_index("section")
    core = section_index % 2
    ring_y = section_index // 2 % 4
    depth = section_index // PLANE
    group_index = section_index // GROUP
    micro_count, row_count, model_width = document_token_embedding.shape
    doc_count = doc_lengths.shape[1]
    doc_span = row_count // doc_count
    decoder_rows = docid_embed.shape[1]
    docid_span = decoder_rows // doc_count
    local_heads = w_enc_qkv.shape[1] // HD
    block_rows = doc_span // 2
    share = docid_span // 2

    index = jnp.arange(row_count)
    doc_there = ring_y ^ (index // block_rows % doc_count)
    place_there = (core ^ (index // (row_count // 2))) * block_rows + index % block_rows
    doc_plain, place_plain = index // doc_span, index % doc_span
    same_there = doc_there[:, None] == doc_there[None, :]
    same_plain = doc_plain[:, None] == doc_plain[None, :]

    def live_rows(doc, place, lengths):
        owner = doc[:, None] == jnp.arange(doc_count)
        return place < jnp.sum(jnp.where(owner, lengths[None, :], 0), axis=1)

    def mix(normed, same, doc, place, lengths):
        projected = jnp.einsum(
            "rd,mcd->mrc", normed, w_enc_qkv, preferred_element_type=jnp.float32
        ).astype(jnp.bfloat16)
        projected = projected.reshape(3, row_count, local_heads, HD)
        allowed = same & live_rows(doc, place, lengths)[None, :]
        return attend(projected[0], projected[1], projected[2], allowed).reshape(row_count, -1)

    own_start = ring_y * doc_span + core * block_rows

    def own_of(m):
        return lax.dynamic_slice_in_dim(document_token_embedding[m], own_start, block_rows, 0)

    def spread(finished):
        own = norm_rows(finished, enc_gain[GROUPS]).astype(jnp.bfloat16)
        arrived = [along_z(own, ((7, to), (6, 5 - to))) for to in range(3)]
        for to in range(3):
            own = jnp.where((depth == to) | (depth == 5 - to), arrived[to], own)
        return gather_rows(own)

    layer_gain = lax.dynamic_index_in_dim(enc_gain, group_index, 0, keepdims=False)
    normed = norm_rows(document_token_embedding[0], enc_gain[0]).astype(jnp.bfloat16)
    mixture = mix(normed, same_plain, doc_plain, place_plain, doc_lengths[0])
    mixture = jnp.take(mixture, doc_there * doc_span + place_there, axis=0)
    current = own_of(0)
    last = micro_count + GROUPS - 2
    onward = [(s, s + GROUP) for s in range(SIZE - GROUP)]
    crossed = [(s, (s ^ PLANE) + GROUP) for s in range(SIZE - GROUP)]
    memories = []
    for step in range(last + 1):
        if step:
            slot = jnp.clip(step - group_index, 0, micro_count - 1)
            lengths = lax.dynamic_index_in_dim(doc_lengths, slot, 0, keepdims=False)
            normed = gather_rows(norm_rows(current, layer_gain).astype(jnp.bfloat16))
            mixture = mix(normed, same_there, doc_there, place_there, lengths)
        term = reduce_ring(mixture, w_enc_out) + 0.5 * current.astype(jnp.float32)
        sent = term.astype(jnp.bfloat16)
        if step >= GROUPS - 1:
            finished = sent.astype(jnp.float32) + exchanged(sent, PLANE).astype(jnp.float32)
            memories.append(spread(finished.astype(jnp.bfloat16)))
        if step < last:
            straight = lax.ppermute(sent, "section", onward).astype(jnp.float32)
            across = lax.ppermute(sent, "section", crossed).astype(jnp.float32)
            current = (straight + across).astype(jnp.bfloat16)
            if step + 1 < micro_count:
                current = jnp.where(group_index == 0, own_of(step + 1), current)

    index = jnp.arange(decoder_rows)
    query_doc = ring_y ^ (index // share % doc_count)
    query_place = (core ^ (index // (decoder_rows // 2))) * share + index % share
    query_order = query_doc * docid_span + query_place
    cross_same = query_doc[:, None] == doc_there[None, :]
    dec_normed = norm_rows(docid_embed, dec_gain[0]).astype(jnp.bfloat16)
    own_queries = jnp.dot(
        dec_normed.reshape(-1, model_width),
        cross_query_key_value_weight[0].T,
        preferred_element_type=jnp.float32,
    ).astype(jnp.bfloat16)
    own_queries = own_queries.reshape(micro_count, decoder_rows, -1, HD)

    mixtures = []
    for m in range(micro_count):
        heads = jnp.einsum(
            "rd,qcd->qrc",
            memories[m],
            cross_query_key_value_weight[1:],
            preferred_element_type=jnp.float32,
        ).astype(jnp.bfloat16)
        heads = heads.reshape(2, row_count, -1, HD)
        allowed = cross_same & live_rows(doc_there, place_there, doc_lengths[m])[None, :]
        queries = jnp.take(own_queries[m], query_order, axis=0)
        mixed = attend(queries, heads[0], heads[1], allowed)
        mixtures.append(mixed.reshape(decoder_rows // share, share, -1))
    cross_mixture = jnp.stack(mixtures, 1).reshape(micro_count * decoder_rows, -1)
    cross_sum = reduce_ring(cross_mixture, w_cross_out)
    for partner in ((1, 0, 3, 2, 5, 4, 7, 6), (7, 2, 1, 4, 3, 6, 5, 0), (3, 6, 5, 0, 7, 2, 1, 4)):
        route = tuple(enumerate(partner))
        cross_sum = add_exchanged(cross_sum, lambda block, route=route: along_z(block, route))
    own_docid = lax.dynamic_slice_in_dim(
        docid_embed, ring_y * docid_span + core * share, share, 1
    ).reshape(micro_count * share, model_width)
    closing_own = norm_rows(own_docid.astype(jnp.float32) + cross_sum, dec_gain[1]).astype(
        jnp.bfloat16
    )
    closing = gather_rows(closing_own)

    scores_here = jnp.dot(closing, docid_head_weight, preferred_element_type=jnp.float32)
    vocab_local = docid_head_weight.shape[1]
    index = jnp.arange(micro_count * decoder_rows)
    micro, doc = index // decoder_rows, index // docid_span % doc_count
    half, row = index // share % 2, index % share
    source = (((half ^ core) * doc_count + (doc ^ ring_y)) * micro_count + micro) * share + row
    scores_vocab = jnp.take(scores_here, source, axis=0).reshape(
        micro_count, decoder_rows, vocab_local
    )
    vocab_start = section_index * vocab_local
    matches = docid_targets[..., None] == vocab_start + jnp.arange(vocab_local)
    sums = jnp.stack(
        [
            jnp.sum(jnp.exp(scores_vocab), axis=-1),
            jnp.sum(jnp.where(matches, scores_vocab, 0.0), axis=-1),
        ]
    ).reshape(1, -1)
    axes = ("section", "rep")
    planes = lax.axis_size("rep")
    size = SIZE * planes
    everything = lax.all_to_all(
        jnp.broadcast_to(sums[None], (size, *sums.shape)), axes, 0, 0, tiled=True
    )
    sums = jnp.sum(everything.reshape(SIZE, planes, -1), axis=0)
    exponent_total, picked = jnp.moveaxis(sums.reshape(planes, 2, -1), 1, 0)
    token_losses = jnp.log(exponent_total) - picked
    token_loss = lax.dynamic_index_in_dim(
        token_losses, lax.axis_index("rep"), 0, keepdims=False
    ).reshape(micro_count, decoder_rows)
    mean_loss = jnp.mean(token_losses)
    return (scores_vocab.astype(jnp.bfloat16), token_loss, mean_loss)


def solution(mesh):
    in_specs = (
        P("rep", None, None),
        P("rep", None),
        P("rep", None, None),
        P("rep", None),
        P(),
        P(),
        P(None, "section", None),
        P("section", None),
        P(None, "section", None),
        P("section", None),
        P(None, "section"),
    )
    out_specs = (P("rep", None, "section"), P("rep", None), P())
    return jax.shard_map(shards, mesh=mesh, in_specs=in_specs, out_specs=out_specs, check_vma=False)
```

```python
import jax
import jax.numpy as jnp
from jax import lax
from jax.sharding import PartitionSpec as P

HD = 64
GROUPS = 4


CORE, PLANE, GROUP = 1, 8, 16
RING = (2, 4, 6)
SIZE = 64


def exchanged(block, mask):
    return lax.ppermute(block, "section", [(s, s ^ mask) for s in range(SIZE)])


def norm_rows(values, gain):
    values = values.astype(jnp.float32)
    scale = lax.rsqrt(jnp.mean(values * values, axis=-1, keepdims=True) + 1e-06)
    return values * scale * gain


def attend(queries, key_rows, values, allowed):
    scores = jnp.einsum("qhe,khe->hqk", queries, key_rows, preferred_element_type=jnp.float32)
    weights = jnp.where(allowed[None], jnp.exp(scores), 0.0)
    probabilities = (weights / jnp.sum(weights, axis=-1, keepdims=True)).astype(jnp.bfloat16)
    mixture = jnp.einsum("hqk,khe->qhe", probabilities, values, preferred_element_type=jnp.float32)
    return mixture.astype(jnp.bfloat16)


def gather_ring(own):
    return jnp.concatenate([own] + [exchanged(own, mask) for mask in RING], 0)


def gather_rows(own):
    ring = gather_ring(own)
    return jnp.concatenate([ring, exchanged(ring, CORE)], 0)


def along_z(block, route):
    pairs = [(z * PLANE + s, to * PLANE + s) for z, to in route for s in range(PLANE)]
    return lax.ppermute(block, "section", pairs)


def reduce_core(mixture, weight):
    half = mixture.shape[0] // 2
    away = jnp.dot(mixture[half:], weight, preferred_element_type=jnp.float32)
    arrived = exchanged(away.astype(jnp.bfloat16), CORE)
    own = jnp.dot(mixture[:half], weight, preferred_element_type=jnp.float32)
    return own + arrived.astype(jnp.float32)


def reduce_ring(ring):
    rows = ring.shape[0] // 4
    sent = ring.astype(jnp.bfloat16)
    total = ring[:rows]
    for k, mask in enumerate(RING):
        block = exchanged(sent[(k + 1) * rows : (k + 2) * rows], mask)
        total = total + block.astype(jnp.float32)
    return total


def add_exchanged(total, exchange):
    return total + exchange(total.astype(jnp.bfloat16)).astype(jnp.float32)


def shards(
    document_token_embedding,
    doc_lengths,
    docid_embed,
    docid_targets,
    enc_gain,
    dec_gain,
    w_enc_qkv,
    w_enc_out,
    cross_query_key_value_weight,
    w_cross_out,
    docid_head_weight,
):
    section_index = lax.axis_index("section")
    core = section_index % 2
    ring_y = section_index // 2 % 4
    depth = section_index // PLANE
    group_index = section_index // GROUP
    micro_count, row_count, model_width = document_token_embedding.shape
    doc_count = doc_lengths.shape[1]
    doc_span = row_count // doc_count
    decoder_rows = docid_embed.shape[1]
    docid_span = decoder_rows // doc_count
    block_rows = doc_span // 2
    share = docid_span // 2

    index = jnp.arange(row_count)
    source_block = (core ^ (index // (row_count // 2))) * 4 + (ring_y ^ (index // block_rows % 4))
    order_there = source_block * block_rows + index % block_rows
    doc_there, place_there = order_there // doc_span, order_there % doc_span
    doc_plain, place_plain = index // doc_span, index % doc_span

    def live_rows(doc, place, lengths):
        owner = doc[:, None] == jnp.arange(doc_count)
        return place < jnp.sum(jnp.where(owner, lengths[None, :], 0), axis=1)

    def mix(normed, maps, doc, place, lengths):
        rows = normed.shape[0]
        projected = jnp.einsum(
            "rd,mcd->mrc", normed, maps, preferred_element_type=jnp.float32
        ).astype(jnp.bfloat16)
        projected = projected.reshape(3, rows, -1, HD)
        allowed = (doc[:, None] == doc[None, :]) & live_rows(doc, place, lengths)[None, :]
        return attend(projected[0], projected[1], projected[2], allowed).reshape(rows, -1)

    maps_other = exchanged(w_enc_qkv, CORE)
    out_other = exchanged(w_enc_out, CORE)
    half = row_count // 2

    own_start = (core * 4 + ring_y) * block_rows

    def own_of(m):
        return lax.dynamic_slice_in_dim(document_token_embedding[m], own_start, block_rows, 0)

    def spread(finished):
        own = norm_rows(finished, enc_gain[GROUPS]).astype(jnp.bfloat16)
        arrived = [along_z(own, ((7, to), (6, 5 - to))) for to in range(3)]
        for to in range(3):
            own = jnp.where((depth == to) | (depth == 5 - to), arrived[to], own)
        return own

    layer_gain = lax.dynamic_index_in_dim(enc_gain, group_index, 0, keepdims=False)
    normed = norm_rows(document_token_embedding[0], enc_gain[0]).astype(jnp.bfloat16)
    mixture = mix(normed, w_enc_qkv, doc_plain, place_plain, doc_lengths[0])
    ring = reduce_core(jnp.take(mixture, order_there, axis=0), w_enc_out)
    current = own_of(0)
    last = micro_count + GROUPS - 2
    onward = [(s, s + GROUP) for s in range(SIZE - GROUP)]
    memories = []
    for step in range(last + 1):
        if step:
            slot = jnp.clip(step - group_index, 0, micro_count - 1)
            lengths = lax.dynamic_index_in_dim(doc_lengths, slot, 0, keepdims=False)
            normed = gather_ring(norm_rows(current, layer_gain).astype(jnp.bfloat16))
            doc, place = doc_there[:half], place_there[:half]
            mixture = mix(normed, w_enc_qkv, doc, place, lengths)
            mixture_other = mix(normed, maps_other, doc, place, lengths)
            if step == last:
                mixture, spread_rows = lax.optimization_barrier((mixture, memories[-1]))
                memories[-1] = spread_rows
            ring = jnp.dot(mixture, w_enc_out, preferred_element_type=jnp.float32)
            ring += jnp.dot(mixture_other, out_other, preferred_element_type=jnp.float32)
        summed = add_exchanged(reduce_ring(ring), lambda block: exchanged(block, PLANE))
        result = (current.astype(jnp.float32) + summed).astype(jnp.bfloat16)
        if step >= GROUPS - 1:
            memories.append(spread(result))
        if step < last:
            current = lax.ppermute(result, "section", onward)
            if step + 1 < micro_count:
                current = jnp.where(group_index == 0, own_of(step + 1), current)
    memories = [gather_rows(rows) for rows in memories]

    index = jnp.arange(decoder_rows)
    query_doc = ring_y ^ (index // share % doc_count)
    query_place = (core ^ (index // (decoder_rows // 2))) * share + index % share
    query_order = query_doc * docid_span + query_place
    cross_same = query_doc[:, None] == doc_there[None, :]
    dec_normed = norm_rows(docid_embed, dec_gain[0]).astype(jnp.bfloat16)
    own_queries = jnp.dot(
        dec_normed.reshape(-1, model_width),
        cross_query_key_value_weight[0].T,
        preferred_element_type=jnp.float32,
    ).astype(jnp.bfloat16)
    own_queries = own_queries.reshape(micro_count, decoder_rows, -1, HD)

    mixtures = []
    for m in range(micro_count):
        heads = jnp.einsum(
            "rd,qcd->qrc",
            memories[m],
            cross_query_key_value_weight[1:],
            preferred_element_type=jnp.float32,
        ).astype(jnp.bfloat16)
        heads = heads.reshape(2, row_count, -1, HD)
        allowed = cross_same & live_rows(doc_there, place_there, doc_lengths[m])[None, :]
        queries = jnp.take(own_queries[m], query_order, axis=0)
        mixed = attend(queries, heads[0], heads[1], allowed)
        mixtures.append(mixed.reshape(decoder_rows // share, share, -1))
    cross_mixture = jnp.stack(mixtures, 1).reshape(micro_count * decoder_rows, -1)
    cross_sum = reduce_ring(reduce_core(cross_mixture, w_cross_out))
    for partner in ((1, 0, 3, 2, 5, 4, 7, 6), (7, 2, 1, 4, 3, 6, 5, 0), (3, 6, 5, 0, 7, 2, 1, 4)):
        route = tuple(enumerate(partner))
        cross_sum = add_exchanged(cross_sum, lambda block, route=route: along_z(block, route))
    own_docid = lax.dynamic_slice_in_dim(
        docid_embed, ring_y * docid_span + core * share, share, 1
    ).reshape(micro_count * share, model_width)
    closing_own = norm_rows(own_docid.astype(jnp.float32) + cross_sum, dec_gain[1]).astype(
        jnp.bfloat16
    )
    closing = gather_rows(closing_own)

    scores_here = jnp.dot(closing, docid_head_weight, preferred_element_type=jnp.float32)
    vocab_local = docid_head_weight.shape[1]
    index = jnp.arange(micro_count * decoder_rows)
    micro, doc = index // decoder_rows, index // docid_span % doc_count
    half, row = index // share % 2, index % share
    source = (((half ^ core) * doc_count + (doc ^ ring_y)) * micro_count + micro) * share + row
    scores_vocab = jnp.take(scores_here, source, axis=0).reshape(
        micro_count, decoder_rows, vocab_local
    )
    vocab_start = section_index * vocab_local
    matches = docid_targets[..., None] == vocab_start + jnp.arange(vocab_local)
    sums = jnp.stack(
        [
            jnp.sum(jnp.exp(scores_vocab), axis=-1),
            jnp.sum(jnp.where(matches, scores_vocab, 0.0), axis=-1),
        ]
    ).reshape(1, -1)
    axes = ("section", "rep")
    planes = lax.axis_size("rep")
    size = SIZE * planes
    everything = lax.all_to_all(
        jnp.broadcast_to(sums[None], (size, *sums.shape)), axes, 0, 0, tiled=True
    )
    sums = jnp.sum(everything.reshape(SIZE, planes, -1), axis=0)
    exponent_total, picked = jnp.moveaxis(sums.reshape(planes, 2, -1), 1, 0)
    token_losses = jnp.log(exponent_total) - picked
    token_loss = lax.dynamic_index_in_dim(
        token_losses, lax.axis_index("rep"), 0, keepdims=False
    ).reshape(micro_count, decoder_rows)
    mean_loss = jnp.mean(token_losses)
    return (scores_vocab.astype(jnp.bfloat16), token_loss, mean_loss)


def solution(mesh):
    in_specs = (
        P("rep", None, None),
        P("rep", None),
        P("rep", None, None),
        P("rep", None),
        P(),
        P(),
        P(None, "section", None),
        P("section", None),
        P(None, "section", None),
        P("section", None),
        P(None, "section"),
    )
    out_specs = (P("rep", None, "section"), P("rep", None), P())
    return jax.shard_map(shards, mesh=mesh, in_specs=in_specs, out_specs=out_specs, check_vma=False)
```

```python
import jax
import jax.numpy as jnp
from jax import lax
from jax.experimental import pallas as pl
from jax.experimental.pallas import tpu as pltpu
from jax.sharding import PartitionSpec as P

HD = 64
GROUPS = 4


CORE, PLANE, GROUP = 1, 8, 16
RING = (2, 4, 6)
SIZE = 64


def exchanged(block, mask):
    return lax.ppermute(block, "section", [(s, s ^ mask) for s in range(SIZE)])


def norm_rows(values, gain):
    values = values.astype(jnp.float32)
    scale = lax.rsqrt(jnp.mean(values * values, axis=-1, keepdims=True) + 1e-06)
    return values * scale * gain


def attend(queries, key_rows, values, allowed):
    scores = jnp.einsum("qhe,khe->hqk", queries, key_rows, preferred_element_type=jnp.float32)
    weights = jnp.where(allowed[None], jnp.exp(scores), 0.0)
    probabilities = (weights / jnp.sum(weights, axis=-1, keepdims=True)).astype(jnp.bfloat16)
    mixture = jnp.einsum("hqk,khe->qhe", probabilities, values, preferred_element_type=jnp.float32)
    return mixture.astype(jnp.bfloat16)


def across(a, b):
    return lax.dot_general(a, b, (((1,), (1,)), ((), ())), preferred_element_type=jnp.float32)


def head_terms(rows, mask, maps_ref, out_ref):
    maps = maps_ref[...]
    projected = across(rows, maps.reshape(3 * HD, maps.shape[2])).astype(jnp.bfloat16)
    queries, key_rows, values = (projected[:, k * HD : (k + 1) * HD] for k in range(3))
    weights = jnp.where(mask > 0.0, jnp.exp(across(queries, key_rows)), 0.0)
    probabilities = (weights / jnp.sum(weights, axis=-1, keepdims=True)).astype(jnp.bfloat16)
    mixture = jnp.dot(probabilities, values, preferred_element_type=jnp.float32)
    return jnp.dot(
        mixture.astype(jnp.bfloat16), out_ref[...], preferred_element_type=jnp.float32
    )


def layer_kernel(
    first, second, third, fourth, mask, maps, maps_other, out, out_other, *outputs_and_scratch
):
    *outputs, rows, total = outputs_and_scratch
    step = pl.program_id(0)
    size = first.shape[0]

    @pl.when(step == 0)
    def _():
        for k, piece in enumerate((first, second, third, fourth)):
            rows[k * size : (k + 1) * size, :] = piece[...]
        total[...] = jnp.zeros_like(total)

    total[...] += head_terms(rows[...], mask[...], maps, out)
    total[...] += head_terms(rows[...], mask[...], maps_other, out_other)

    @pl.when(step == pl.num_programs(0) - 1)
    def _():
        for k, output in enumerate(outputs):
            output[...] = total[k * size : (k + 1) * size, :].astype(output.dtype)


def layer_terms(pieces, allowed, maps, maps_other, out, out_other):
    size, width = pieces[0].shape
    whole = pl.BlockSpec(memory_space=pltpu.VMEM)
    maps_spec = pl.BlockSpec((3, HD, width), lambda h: (0, h, 0))
    out_spec = pl.BlockSpec((HD, width), lambda h: (h, 0))
    types = [jnp.float32] + [jnp.bfloat16] * 3
    return pl.pallas_call(
        layer_kernel,
        grid=(maps.shape[1] // HD,),
        in_specs=[whole] * 5 + [maps_spec, maps_spec, out_spec, out_spec],
        out_specs=[whole] * 4,
        out_shape=[jax.ShapeDtypeStruct((size, width), dtype) for dtype in types],
        scratch_shapes=[
            pltpu.VMEM((4 * size, width), jnp.bfloat16),
            pltpu.VMEM((4 * size, width), jnp.float32),
        ],
        compiler_params=pltpu.CompilerParams(vmem_limit_bytes=24 * 1024 * 1024),
        cost_estimate=pl.CostEstimate(
            flops=16 * size * width * maps.shape[1] * 4,
            bytes_accessed=16 * maps.shape[1] * width,
            transcendentals=0,
        ),
    )(*pieces, allowed.astype(jnp.float32), maps, maps_other, out, out_other)


def ring_pieces(own):
    return [own] + [exchanged(own, mask) for mask in RING]


def gather_rows(own):
    ring = jnp.concatenate(ring_pieces(own), 0)
    return jnp.concatenate([ring, exchanged(ring, CORE)], 0)


def along_z(block, route):
    pairs = [(z * PLANE + s, to * PLANE + s) for z, to in route for s in range(PLANE)]
    return lax.ppermute(block, "section", pairs)


def reduce_core(mixture, weight):
    half = mixture.shape[0] // 2
    away = jnp.dot(mixture[half:], weight, preferred_element_type=jnp.float32)
    arrived = exchanged(away.astype(jnp.bfloat16), CORE)
    own = jnp.dot(mixture[:half], weight, preferred_element_type=jnp.float32)
    return own + arrived.astype(jnp.float32)


def ring_blocks(ring):
    rows = ring.shape[0] // 4
    sent = ring.astype(jnp.bfloat16)
    return [ring[:rows]] + [sent[k * rows : (k + 1) * rows] for k in range(1, 4)]


def reduce_ring(total, *blocks):
    for mask, block in zip(RING, blocks):
        total = total + exchanged(block, mask).astype(jnp.float32)
    return total


def add_exchanged(total, exchange):
    return total + exchange(total.astype(jnp.bfloat16)).astype(jnp.float32)


def shards(
    document_token_embedding,
    doc_lengths,
    docid_embed,
    docid_targets,
    enc_gain,
    dec_gain,
    w_enc_qkv,
    w_enc_out,
    cross_query_key_value_weight,
    w_cross_out,
    docid_head_weight,
):
    section_index = lax.axis_index("section")
    core = section_index % 2
    ring_y = section_index // 2 % 4
    depth = section_index // PLANE
    group_index = section_index // GROUP
    micro_count, row_count, model_width = document_token_embedding.shape
    doc_count = doc_lengths.shape[1]
    doc_span = row_count // doc_count
    decoder_rows = docid_embed.shape[1]
    docid_span = decoder_rows // doc_count
    block_rows = doc_span // 2
    share = docid_span // 2

    index = jnp.arange(row_count)
    source_block = (core ^ (index // (row_count // 2))) * 4 + (ring_y ^ (index // block_rows % 4))
    order_there = source_block * block_rows + index % block_rows
    doc_there, place_there = order_there // doc_span, order_there % doc_span
    doc_plain, place_plain = index // doc_span, index % doc_span

    def live_rows(doc, place, lengths):
        owner = doc[:, None] == jnp.arange(doc_count)
        return place < jnp.sum(jnp.where(owner, lengths[None, :], 0), axis=1)

    def mix(normed, maps, doc, place, lengths):
        rows = normed.shape[0]
        projected = jnp.einsum(
            "rd,mcd->mrc", normed, maps, preferred_element_type=jnp.float32
        ).astype(jnp.bfloat16)
        projected = projected.reshape(3, rows, -1, HD)
        allowed = (doc[:, None] == doc[None, :]) & live_rows(doc, place, lengths)[None, :]
        return attend(projected[0], projected[1], projected[2], allowed).reshape(rows, -1)

    maps_other = exchanged(w_enc_qkv, CORE)
    out_other = exchanged(w_enc_out, CORE)
    half = row_count // 2

    own_start = (core * 4 + ring_y) * block_rows

    def own_of(m):
        return lax.dynamic_slice_in_dim(document_token_embedding[m], own_start, block_rows, 0)

    def spread(finished):
        own = norm_rows(finished, enc_gain[GROUPS]).astype(jnp.bfloat16)
        arrived = [along_z(own, ((7, to), (6, 5 - to))) for to in range(3)]
        for to in range(3):
            own = jnp.where((depth == to) | (depth == 5 - to), arrived[to], own)
        return own

    layer_gain = lax.dynamic_index_in_dim(enc_gain, group_index, 0, keepdims=False)
    normed = norm_rows(document_token_embedding[0], enc_gain[0]).astype(jnp.bfloat16)
    mixture = mix(normed, w_enc_qkv, doc_plain, place_plain, doc_lengths[0])
    blocks = ring_blocks(reduce_core(jnp.take(mixture, order_there, axis=0), w_enc_out))
    current = own_of(0)
    last = micro_count + GROUPS - 2
    onward = [(s, s + GROUP) for s in range(SIZE - GROUP)]
    memories = []
    for step in range(last + 1):
        if step:
            slot = jnp.clip(step - group_index, 0, micro_count - 1)
            lengths = lax.dynamic_index_in_dim(doc_lengths, slot, 0, keepdims=False)
            pieces = ring_pieces(norm_rows(current, layer_gain).astype(jnp.bfloat16))
            doc, place = doc_there[:half], place_there[:half]
            allowed = (doc[:, None] == doc[None, :]) & live_rows(doc, place, lengths)[None, :]
            blocks = layer_terms(pieces, allowed, w_enc_qkv, maps_other, w_enc_out, out_other)
            if step == last:
                blocks, memories[-1] = lax.optimization_barrier((blocks, memories[-1]))
        summed = add_exchanged(reduce_ring(*blocks), lambda block: exchanged(block, PLANE))
        result = (current.astype(jnp.float32) + summed).astype(jnp.bfloat16)
        if step >= GROUPS - 1:
            memories.append(spread(result))
        if step < last:
            current = lax.ppermute(result, "section", onward)
            if step + 1 < micro_count:
                current = jnp.where(group_index == 0, own_of(step + 1), current)
    memories = [gather_rows(rows) for rows in memories]

    index = jnp.arange(decoder_rows)
    query_doc = ring_y ^ (index // share % doc_count)
    query_place = (core ^ (index // (decoder_rows // 2))) * share + index % share
    query_order = query_doc * docid_span + query_place
    cross_same = query_doc[:, None] == doc_there[None, :]
    dec_normed = norm_rows(docid_embed, dec_gain[0]).astype(jnp.bfloat16)
    own_queries = jnp.dot(
        dec_normed.reshape(-1, model_width),
        cross_query_key_value_weight[0].T,
        preferred_element_type=jnp.float32,
    ).astype(jnp.bfloat16)
    own_queries = own_queries.reshape(micro_count, decoder_rows, -1, HD)

    mixtures = []
    for m in range(micro_count):
        heads = jnp.einsum(
            "rd,qcd->qrc",
            memories[m],
            cross_query_key_value_weight[1:],
            preferred_element_type=jnp.float32,
        ).astype(jnp.bfloat16)
        heads = heads.reshape(2, row_count, -1, HD)
        allowed = cross_same & live_rows(doc_there, place_there, doc_lengths[m])[None, :]
        queries = jnp.take(own_queries[m], query_order, axis=0)
        mixed = attend(queries, heads[0], heads[1], allowed)
        mixtures.append(mixed.reshape(decoder_rows // share, share, -1))
    cross_mixture = jnp.stack(mixtures, 1).reshape(micro_count * decoder_rows, -1)
    cross_sum = reduce_ring(*ring_blocks(reduce_core(cross_mixture, w_cross_out)))
    for partner in ((1, 0, 3, 2, 5, 4, 7, 6), (7, 2, 1, 4, 3, 6, 5, 0), (3, 6, 5, 0, 7, 2, 1, 4)):
        route = tuple(enumerate(partner))
        cross_sum = add_exchanged(cross_sum, lambda block, route=route: along_z(block, route))
    own_docid = lax.dynamic_slice_in_dim(
        docid_embed, ring_y * docid_span + core * share, share, 1
    ).reshape(micro_count * share, model_width)
    closing_own = norm_rows(own_docid.astype(jnp.float32) + cross_sum, dec_gain[1]).astype(
        jnp.bfloat16
    )
    closing = gather_rows(closing_own)

    scores_here = jnp.dot(closing, docid_head_weight, preferred_element_type=jnp.float32)
    vocab_local = docid_head_weight.shape[1]
    index = jnp.arange(micro_count * decoder_rows)
    micro, doc = index // decoder_rows, index // docid_span % doc_count
    half, row = index // share % 2, index % share
    source = (((half ^ core) * doc_count + (doc ^ ring_y)) * micro_count + micro) * share + row
    scores_vocab = jnp.take(scores_here, source, axis=0).reshape(
        micro_count, decoder_rows, vocab_local
    )
    vocab_start = section_index * vocab_local
    matches = docid_targets[..., None] == vocab_start + jnp.arange(vocab_local)
    sums = jnp.stack(
        [
            jnp.sum(jnp.exp(scores_vocab), axis=-1),
            jnp.sum(jnp.where(matches, scores_vocab, 0.0), axis=-1),
        ]
    ).reshape(1, -1)
    axes = ("section", "rep")
    planes = lax.axis_size("rep")
    size = SIZE * planes
    everything = lax.all_to_all(
        jnp.broadcast_to(sums[None], (size, *sums.shape)), axes, 0, 0, tiled=True
    )
    sums = jnp.sum(everything.reshape(SIZE, planes, -1), axis=0)
    exponent_total, picked = jnp.moveaxis(sums.reshape(planes, 2, -1), 1, 0)
    token_losses = jnp.log(exponent_total) - picked
    token_loss = lax.dynamic_index_in_dim(
        token_losses, lax.axis_index("rep"), 0, keepdims=False
    ).reshape(micro_count, decoder_rows)
    mean_loss = jnp.mean(token_losses)
    return (scores_vocab.astype(jnp.bfloat16), token_loss, mean_loss)


def solution(mesh):
    in_specs = (
        P("rep", None, None),
        P("rep", None),
        P("rep", None, None),
        P("rep", None),
        P(),
        P(),
        P(None, "section", None),
        P("section", None),
        P(None, "section", None),
        P("section", None),
        P(None, "section"),
    )
    out_specs = (P("rep", None, "section"), P("rep", None), P())
    return jax.shard_map(shards, mesh=mesh, in_specs=in_specs, out_specs=out_specs, check_vma=False)
```

```python
import jax
import jax.numpy as jnp
from jax import lax
from jax.experimental import pallas as pl
from jax.experimental.pallas import tpu as pltpu
from jax.sharding import PartitionSpec as P

HD = 64
GROUPS = 4


CORE, PLANE, GROUP = 1, 8, 16
RING = (2, 4, 6)
SIZE = 64
VMEM_LIMIT = 48 * 1024 * 1024


def exchanged(block, mask):
    return lax.ppermute(block, "section", [(s, s ^ mask) for s in range(SIZE)])


def norm_rows(values, gain):
    values = values.astype(jnp.float32)
    scale = lax.rsqrt(jnp.mean(values * values, axis=-1, keepdims=True) + 1e-06)
    return values * scale * gain


def attend(queries, key_rows, values, allowed):
    scores = jnp.einsum("qhe,khe->hqk", queries, key_rows, preferred_element_type=jnp.float32)
    weights = jnp.where(allowed[None], jnp.exp(scores), 0.0)
    probabilities = (weights / jnp.sum(weights, axis=-1, keepdims=True)).astype(jnp.bfloat16)
    mixture = jnp.einsum("hqk,khe->qhe", probabilities, values, preferred_element_type=jnp.float32)
    return mixture.astype(jnp.bfloat16)


def across(a, b):
    return lax.dot_general(a, b, (((1,), (1,)), ((), ())), preferred_element_type=jnp.float32)


def head_mixtures(projected, mask):
    mixtures = []
    for low in range(0, projected[0].shape[1], HD):
        queries, key_rows, values = (columns[:, low : low + HD] for columns in projected)
        weights = jnp.where(mask > 0.0, jnp.exp(across(queries, key_rows)), 0.0)
        probabilities = (weights / jnp.sum(weights, axis=-1, keepdims=True)).astype(jnp.bfloat16)
        mixtures.append(jnp.dot(probabilities, values, preferred_element_type=jnp.float32))
    return jnp.concatenate(mixtures, 1).astype(jnp.bfloat16)


def layer_kernel(first, second, third, fourth, mask, *refs):
    sources, outputs, held, sems = refs[:4], refs[4:8], refs[8:12], refs[12]
    size = first.shape[0]
    copies = []
    for array in (0, 1):
        for member in range(3):
            copies.append(
                pltpu.make_async_copy(
                    sources[array].at[member], held[array].at[member], sems.at[len(copies)]
                )
            )
    for array in (2, 3):
        copies.append(pltpu.make_async_copy(sources[array], held[array], sems.at[len(copies)]))
    for copy in copies:
        copy.start()
    rows = jnp.concatenate([piece[...] for piece in (first, second, third, fourth)], 0)
    projected = []
    for array in (0, 1):
        for member in range(3):
            copies[3 * array + member].wait()
        pj = across(rows, held[array][...].reshape(576, 4096)).astype(jnp.bfloat16)
        projected += [pj[:, :192], pj[:, 192:384], pj[:, 384:]]
    mixed = [head_mixtures(projected[3 * k : 3 * k + 3], mask[...]) for k in (0, 1)]
    copies[6].wait()
    copies[7].wait()
    total = jnp.dot(mixed[0], held[2][...], preferred_element_type=jnp.float32)
    total += jnp.dot(mixed[1], held[3][...], preferred_element_type=jnp.float32)
    for k, output in enumerate(outputs):
        output[...] = total[k * size : (k + 1) * size, :].astype(output.dtype)


def layer_terms(pieces, allowed, maps, maps_other, out, out_other):
    size, width = pieces[0].shape
    whole = pl.BlockSpec(memory_space=pltpu.VMEM)
    types = [jnp.float32] + [jnp.bfloat16] * 3
    return pl.pallas_call(
        layer_kernel,
        in_specs=[whole] * 5 + [pl.BlockSpec(memory_space=pl.ANY)] * 4,
        out_specs=[whole] * 4,
        out_shape=[jax.ShapeDtypeStruct((size, width), dtype) for dtype in types],
        scratch_shapes=[pltpu.VMEM(a.shape, a.dtype) for a in (maps, maps_other, out, out_other)]
        + [pltpu.SemaphoreType.DMA((8,))],
        compiler_params=pltpu.CompilerParams(vmem_limit_bytes=VMEM_LIMIT),
        cost_estimate=pl.CostEstimate(
            flops=16 * size * width * maps.shape[1] * 4,
            bytes_accessed=16 * maps.shape[1] * width,
            transcendentals=0,
        ),
    )(*pieces, allowed.astype(jnp.float32), maps, maps_other, out, out_other)


def ring_pieces(own):
    return [own] + [exchanged(own, mask) for mask in RING]


def gather_rows(own):
    ring = jnp.concatenate(ring_pieces(own), 0)
    return jnp.concatenate([ring, exchanged(ring, CORE)], 0)


def along_z(block, route):
    pairs = [(z * PLANE + s, to * PLANE + s) for z, to in route for s in range(PLANE)]
    return lax.ppermute(block, "section", pairs)


def reduce_core(mixture, weight):
    half = mixture.shape[0] // 2
    away = jnp.dot(mixture[half:], weight, preferred_element_type=jnp.float32)
    arrived = exchanged(away.astype(jnp.bfloat16), CORE)
    own = jnp.dot(mixture[:half], weight, preferred_element_type=jnp.float32)
    return own + arrived.astype(jnp.float32)


def ring_blocks(ring):
    rows = ring.shape[0] // 4
    sent = ring.astype(jnp.bfloat16)
    return [ring[:rows]] + [sent[k * rows : (k + 1) * rows] for k in range(1, 4)]


def reduce_ring(total, *blocks):
    for mask, block in zip(RING, blocks):
        total = total + exchanged(block, mask).astype(jnp.float32)
    return total


def add_exchanged(total, exchange):
    return total + exchange(total.astype(jnp.bfloat16)).astype(jnp.float32)


def shards(
    document_token_embedding,
    doc_lengths,
    docid_embed,
    docid_targets,
    enc_gain,
    dec_gain,
    w_enc_qkv,
    w_enc_out,
    cross_query_key_value_weight,
    w_cross_out,
    docid_head_weight,
):
    section_index = lax.axis_index("section")
    core = section_index % 2
    ring_y = section_index // 2 % 4
    depth = section_index // PLANE
    group_index = section_index // GROUP
    micro_count, row_count, model_width = document_token_embedding.shape
    doc_count = doc_lengths.shape[1]
    doc_span = row_count // doc_count
    decoder_rows = docid_embed.shape[1]
    docid_span = decoder_rows // doc_count
    block_rows = doc_span // 2
    share = docid_span // 2

    index = jnp.arange(row_count)
    source_block = (core ^ (index // (row_count // 2))) * 4 + (ring_y ^ (index // block_rows % 4))
    order_there = source_block * block_rows + index % block_rows
    doc_there, place_there = order_there // doc_span, order_there % doc_span
    doc_plain, place_plain = index // doc_span, index % doc_span

    def live_rows(doc, place, lengths):
        owner = doc[:, None] == jnp.arange(doc_count)
        return place < jnp.sum(jnp.where(owner, lengths[None, :], 0), axis=1)

    def mix(normed, maps, doc, place, lengths):
        rows = normed.shape[0]
        projected = jnp.einsum(
            "rd,mcd->mrc", normed, maps, preferred_element_type=jnp.float32
        ).astype(jnp.bfloat16)
        projected = projected.reshape(3, rows, -1, HD)
        allowed = (doc[:, None] == doc[None, :]) & live_rows(doc, place, lengths)[None, :]
        return attend(projected[0], projected[1], projected[2], allowed).reshape(rows, -1)

    maps_other = exchanged(w_enc_qkv, CORE)
    out_other = exchanged(w_enc_out, CORE)
    half = row_count // 2

    own_start = (core * 4 + ring_y) * block_rows

    def own_of(m):
        return lax.dynamic_slice_in_dim(document_token_embedding[m], own_start, block_rows, 0)

    def spread(finished):
        own = norm_rows(finished, enc_gain[GROUPS]).astype(jnp.bfloat16)
        arrived = [along_z(own, ((7, to), (6, 5 - to))) for to in range(3)]
        for to in range(3):
            own = jnp.where((depth == to) | (depth == 5 - to), arrived[to], own)
        return own

    layer_gain = lax.dynamic_index_in_dim(enc_gain, group_index, 0, keepdims=False)
    normed = norm_rows(document_token_embedding[0], enc_gain[0]).astype(jnp.bfloat16)
    mixture = mix(normed, w_enc_qkv, doc_plain, place_plain, doc_lengths[0])
    blocks = ring_blocks(reduce_core(jnp.take(mixture, order_there, axis=0), w_enc_out))
    current = own_of(0)
    last = micro_count + GROUPS - 2
    onward = [(s, s + GROUP) for s in range(SIZE - GROUP)]
    memories = []
    for step in range(last + 1):
        if step:
            slot = jnp.clip(step - group_index, 0, micro_count - 1)
            lengths = lax.dynamic_index_in_dim(doc_lengths, slot, 0, keepdims=False)
            pieces = ring_pieces(norm_rows(current, layer_gain).astype(jnp.bfloat16))
            doc, place = doc_there[:half], place_there[:half]
            allowed = (doc[:, None] == doc[None, :]) & live_rows(doc, place, lengths)[None, :]
            blocks = layer_terms(pieces, allowed, w_enc_qkv, maps_other, w_enc_out, out_other)
            if step == last:
                blocks, memories[-1] = lax.optimization_barrier((blocks, memories[-1]))
        summed = add_exchanged(reduce_ring(*blocks), lambda block: exchanged(block, PLANE))
        result = (current.astype(jnp.float32) + summed).astype(jnp.bfloat16)
        if step >= GROUPS - 1:
            memories.append(spread(result))
        if step < last:
            current = lax.ppermute(result, "section", onward)
            if step + 1 < micro_count:
                current = jnp.where(group_index == 0, own_of(step + 1), current)
    memories = [gather_rows(rows) for rows in memories]

    index = jnp.arange(decoder_rows)
    query_doc = ring_y ^ (index // share % doc_count)
    query_place = (core ^ (index // (decoder_rows // 2))) * share + index % share
    query_order = query_doc * docid_span + query_place
    cross_same = query_doc[:, None] == doc_there[None, :]
    dec_normed = norm_rows(docid_embed, dec_gain[0]).astype(jnp.bfloat16)
    own_queries = jnp.dot(
        dec_normed.reshape(-1, model_width),
        cross_query_key_value_weight[0].T,
        preferred_element_type=jnp.float32,
    ).astype(jnp.bfloat16)
    own_queries = own_queries.reshape(micro_count, decoder_rows, -1, HD)

    mixtures = []
    for m in range(micro_count):
        heads = jnp.einsum(
            "rd,qcd->qrc",
            memories[m],
            cross_query_key_value_weight[1:],
            preferred_element_type=jnp.float32,
        ).astype(jnp.bfloat16)
        heads = heads.reshape(2, row_count, -1, HD)
        allowed = cross_same & live_rows(doc_there, place_there, doc_lengths[m])[None, :]
        queries = jnp.take(own_queries[m], query_order, axis=0)
        mixed = attend(queries, heads[0], heads[1], allowed)
        mixtures.append(mixed.reshape(decoder_rows // share, share, -1))
    cross_mixture = jnp.stack(mixtures, 1).reshape(micro_count * decoder_rows, -1)
    cross_sum = reduce_ring(*ring_blocks(reduce_core(cross_mixture, w_cross_out)))
    for partner in ((1, 0, 3, 2, 5, 4, 7, 6), (7, 2, 1, 4, 3, 6, 5, 0), (3, 6, 5, 0, 7, 2, 1, 4)):
        route = tuple(enumerate(partner))
        cross_sum = add_exchanged(cross_sum, lambda block, route=route: along_z(block, route))
    own_docid = lax.dynamic_slice_in_dim(
        docid_embed, ring_y * docid_span + core * share, share, 1
    ).reshape(micro_count * share, model_width)
    closing_own = norm_rows(own_docid.astype(jnp.float32) + cross_sum, dec_gain[1]).astype(
        jnp.bfloat16
    )
    closing = gather_rows(closing_own)

    scores_here = jnp.dot(closing, docid_head_weight, preferred_element_type=jnp.float32)
    vocab_local = docid_head_weight.shape[1]
    index = jnp.arange(micro_count * decoder_rows)
    micro, doc = index // decoder_rows, index // docid_span % doc_count
    half, row = index // share % 2, index % share
    source = (((half ^ core) * doc_count + (doc ^ ring_y)) * micro_count + micro) * share + row
    scores_vocab = jnp.take(scores_here, source, axis=0).reshape(
        micro_count, decoder_rows, vocab_local
    )
    vocab_start = section_index * vocab_local
    matches = docid_targets[..., None] == vocab_start + jnp.arange(vocab_local)
    sums = jnp.stack(
        [
            jnp.sum(jnp.exp(scores_vocab), axis=-1),
            jnp.sum(jnp.where(matches, scores_vocab, 0.0), axis=-1),
        ]
    ).reshape(1, -1)
    axes = ("section", "rep")
    planes = lax.axis_size("rep")
    size = SIZE * planes
    everything = lax.all_to_all(
        jnp.broadcast_to(sums[None], (size, *sums.shape)), axes, 0, 0, tiled=True
    )
    sums = jnp.sum(everything.reshape(SIZE, planes, -1), axis=0)
    exponent_total, picked = jnp.moveaxis(sums.reshape(planes, 2, -1), 1, 0)
    token_losses = jnp.log(exponent_total) - picked
    token_loss = lax.dynamic_index_in_dim(
        token_losses, lax.axis_index("rep"), 0, keepdims=False
    ).reshape(micro_count, decoder_rows)
    mean_loss = jnp.mean(token_losses)
    return (scores_vocab.astype(jnp.bfloat16), token_loss, mean_loss)


def solution(mesh):
    in_specs = (
        P("rep", None, None),
        P("rep", None),
        P("rep", None, None),
        P("rep", None),
        P(),
        P(),
        P(None, "section", None),
        P("section", None),
        P(None, "section", None),
        P("section", None),
        P(None, "section"),
    )
    out_specs = (P("rep", None, "section"), P("rep", None), P())
    return jax.shard_map(shards, mesh=mesh, in_specs=in_specs, out_specs=out_specs, check_vma=False)
```

```python
import jax
import jax.numpy as jnp
from jax import lax
from jax.experimental import pallas as pl
from jax.experimental.pallas import tpu as pltpu
from jax.sharding import PartitionSpec as P

HD = 64
GROUPS = 4


CORE, PLANE, GROUP = 1, 8, 16
RING = (2, 4, 6)
SIZE = 64
VMEM_LIMIT = 48 * 1024 * 1024


def exchanged(block, mask):
    return lax.ppermute(block, "section", [(s, s ^ mask) for s in range(SIZE)])


def norm_rows(values, gain):
    values = values.astype(jnp.float32)
    scale = lax.rsqrt(jnp.mean(values * values, axis=-1, keepdims=True) + 1e-06)
    return values * scale * gain


def attend(queries, key_rows, values, allowed):
    scores = jnp.einsum("qhe,khe->hqk", queries, key_rows, preferred_element_type=jnp.float32)
    weights = jnp.where(allowed[None], jnp.exp(scores), 0.0)
    probabilities = (weights / jnp.sum(weights, axis=-1, keepdims=True)).astype(jnp.bfloat16)
    mixture = jnp.einsum("hqk,khe->qhe", probabilities, values, preferred_element_type=jnp.float32)
    return mixture.astype(jnp.bfloat16)


def across(a, b):
    return lax.dot_general(a, b, (((1,), (1,)), ((), ())), preferred_element_type=jnp.float32)


def head_mixtures(projected, mask):
    mixtures = []
    for low in range(0, projected[0].shape[1], HD):
        queries, key_rows, values = (columns[:, low : low + HD] for columns in projected)
        weights = jnp.where(mask > 0.0, jnp.exp(across(queries, key_rows)), 0.0)
        probabilities = (weights / jnp.sum(weights, axis=-1, keepdims=True)).astype(jnp.bfloat16)
        mixtures.append(jnp.dot(probabilities, values, preferred_element_type=jnp.float32))
    return jnp.concatenate(mixtures, 1).astype(jnp.bfloat16)


def layer_kernel(first, second, third, fourth, mask, *refs):
    sources, outputs, held, sems = refs[:4], refs[4:8], refs[8:12], refs[12]
    size = first.shape[0]
    copies = []
    for array in (0, 1):
        for member in range(3):
            copies.append(
                pltpu.make_async_copy(
                    sources[array].at[member], held[array].at[member], sems.at[len(copies)]
                )
            )
    for array in (2, 3):
        copies.append(pltpu.make_async_copy(sources[array], held[array], sems.at[len(copies)]))
    for copy in copies:
        copy.start()
    rows = jnp.concatenate([piece[...] for piece in (first, second, third, fourth)], 0)
    projected = []
    for array in (0, 1):
        for member in range(3):
            copies[3 * array + member].wait()
        pj = across(rows, held[array][...].reshape(576, 4096)).astype(jnp.bfloat16)
        projected += [pj[:, :192], pj[:, 192:384], pj[:, 384:]]
    mixed = [head_mixtures(projected[3 * k : 3 * k + 3], mask[...]) for k in (0, 1)]
    copies[6].wait()
    copies[7].wait()
    total = jnp.dot(mixed[0], held[2][...], preferred_element_type=jnp.float32)
    total += jnp.dot(mixed[1], held[3][...], preferred_element_type=jnp.float32)
    for k, output in enumerate(outputs):
        output[...] = total[k * size : (k + 1) * size, :].astype(output.dtype)


def layer_terms(pieces, allowed, maps, maps_other, out, out_other):
    size, width = pieces[0].shape
    whole = pl.BlockSpec(memory_space=pltpu.VMEM)
    types = [jnp.float32] + [jnp.bfloat16] * 3
    return pl.pallas_call(
        layer_kernel,
        in_specs=[whole] * 5 + [pl.BlockSpec(memory_space=pl.ANY)] * 4,
        out_specs=[whole] * 4,
        out_shape=[jax.ShapeDtypeStruct((size, width), dtype) for dtype in types],
        scratch_shapes=[pltpu.VMEM(a.shape, a.dtype) for a in (maps, maps_other, out, out_other)]
        + [pltpu.SemaphoreType.DMA((8,))],
        compiler_params=pltpu.CompilerParams(vmem_limit_bytes=VMEM_LIMIT),
        cost_estimate=pl.CostEstimate(
            flops=16 * size * width * maps.shape[1] * 4,
            bytes_accessed=16 * maps.shape[1] * width,
            transcendentals=0,
        ),
    )(*pieces, allowed.astype(jnp.float32), maps, maps_other, out, out_other)


def first_kernel(place, gain, mask, documents, maps, out, own, away, held, maps_held, out_held, total, sems):
    copies = [
        pltpu.make_async_copy(documents.at[0], held, sems.at[0]),
        pltpu.make_async_copy(maps, maps_held, sems.at[1]),
        pltpu.make_async_copy(out, out_held, sems.at[2]),
    ]
    for copy in copies:
        copy.start()
    copies[0].wait()
    rows = norm_rows(held[...], gain[...]).astype(jnp.bfloat16)
    copies[1].wait()
    columns = maps_held.shape[1]
    projected = across(rows, maps_held[...].reshape(3 * columns, rows.shape[1]))
    projected = projected.astype(jnp.bfloat16)
    members = [projected[:, k * columns : (k + 1) * columns] for k in range(3)]
    mixed = head_mixtures(members, mask[...])
    copies[2].wait()
    total[...] = jnp.dot(mixed, out_held[...], preferred_element_type=jnp.float32)
    core, ring_y = place[0], place[1]
    half = own.shape[0]
    size = half // 4
    for k in range(4):
        there = (ring_y ^ k) * size
        here = pl.ds(pl.multiple_of(core * half + there, size), size)
        other = pl.ds(pl.multiple_of((1 - core) * half + there, size), size)
        own[k * size : (k + 1) * size, :] = total[here, :]
        away[k * size : (k + 1) * size, :] = total[other, :].astype(away.dtype)


def first_terms(place, gain, allowed, documents, maps, out):
    _, count, width = documents.shape
    whole = pl.BlockSpec(memory_space=pltpu.VMEM)
    large = pl.BlockSpec(memory_space=pl.ANY)
    return pl.pallas_call(
        first_kernel,
        in_specs=[pl.BlockSpec(memory_space=pltpu.SMEM), whole, whole, large, large, large],
        out_specs=[whole, whole],
        out_shape=[
            jax.ShapeDtypeStruct((count // 2, width), jnp.float32),
            jax.ShapeDtypeStruct((count // 2, width), jnp.bfloat16),
        ],
        scratch_shapes=[
            pltpu.VMEM((count, width), documents.dtype),
            pltpu.VMEM(maps.shape, maps.dtype),
            pltpu.VMEM(out.shape, out.dtype),
            pltpu.VMEM((count, width), jnp.float32),
            pltpu.SemaphoreType.DMA((3,)),
        ],
        compiler_params=pltpu.CompilerParams(vmem_limit_bytes=VMEM_LIMIT),
        cost_estimate=pl.CostEstimate(
            flops=8 * count * width * maps.shape[1],
            bytes_accessed=8 * maps.shape[1] * width,
            transcendentals=0,
        ),
    )(place, gain, allowed.astype(jnp.float32), documents, maps, out)


def ring_pieces(own):
    return [own] + [exchanged(own, mask) for mask in RING]


def gather_rows(own):
    ring = jnp.concatenate(ring_pieces(own), 0)
    return jnp.concatenate([ring, exchanged(ring, CORE)], 0)


def along_z(block, route):
    pairs = [(z * PLANE + s, to * PLANE + s) for z, to in route for s in range(PLANE)]
    return lax.ppermute(block, "section", pairs)


def reduce_core(mixture, weight):
    half = mixture.shape[0] // 2
    away = jnp.dot(mixture[half:], weight, preferred_element_type=jnp.float32)
    arrived = exchanged(away.astype(jnp.bfloat16), CORE)
    own = jnp.dot(mixture[:half], weight, preferred_element_type=jnp.float32)
    return own + arrived.astype(jnp.float32)


def ring_blocks(ring):
    rows = ring.shape[0] // 4
    sent = ring.astype(jnp.bfloat16)
    return [ring[:rows]] + [sent[k * rows : (k + 1) * rows] for k in range(1, 4)]


def reduce_ring(total, *blocks):
    for mask, block in zip(RING, blocks):
        total = total + exchanged(block, mask).astype(jnp.float32)
    return total


def add_exchanged(total, exchange):
    return total + exchange(total.astype(jnp.bfloat16)).astype(jnp.float32)


def shards(
    document_token_embedding,
    doc_lengths,
    docid_embed,
    docid_targets,
    enc_gain,
    dec_gain,
    w_enc_qkv,
    w_enc_out,
    cross_query_key_value_weight,
    w_cross_out,
    docid_head_weight,
):
    section_index = lax.axis_index("section")
    core = section_index % 2
    ring_y = section_index // 2 % 4
    depth = section_index // PLANE
    group_index = section_index // GROUP
    micro_count, row_count, model_width = document_token_embedding.shape
    doc_count = doc_lengths.shape[1]
    doc_span = row_count // doc_count
    decoder_rows = docid_embed.shape[1]
    docid_span = decoder_rows // doc_count
    block_rows = doc_span // 2
    share = docid_span // 2

    index = jnp.arange(row_count)
    source_block = (core ^ (index // (row_count // 2))) * 4 + (ring_y ^ (index // block_rows % 4))
    order_there = source_block * block_rows + index % block_rows
    doc_there, place_there = order_there // doc_span, order_there % doc_span
    doc_plain, place_plain = index // doc_span, index % doc_span

    def live_rows(doc, place, lengths):
        owner = doc[:, None] == jnp.arange(doc_count)
        return place < jnp.sum(jnp.where(owner, lengths[None, :], 0), axis=1)

    maps_other = exchanged(w_enc_qkv, CORE)
    out_other = exchanged(w_enc_out, CORE)
    half = row_count // 2

    own_start = (core * 4 + ring_y) * block_rows

    def own_of(m):
        return lax.dynamic_slice_in_dim(document_token_embedding[m], own_start, block_rows, 0)

    def spread(finished):
        own = norm_rows(finished, enc_gain[GROUPS]).astype(jnp.bfloat16)
        arrived = [along_z(own, ((7, to), (6, 5 - to))) for to in range(3)]
        for to in range(3):
            own = jnp.where((depth == to) | (depth == 5 - to), arrived[to], own)
        return own

    layer_gain = lax.dynamic_index_in_dim(enc_gain, group_index, 0, keepdims=False)
    allowed = doc_plain[:, None] == doc_plain[None, :]
    allowed = allowed & live_rows(doc_plain, place_plain, doc_lengths[0])[None, :]
    own_half, away_half = first_terms(
        jnp.stack([core, ring_y]).astype(jnp.int32),
        enc_gain[:1],
        allowed,
        document_token_embedding,
        w_enc_qkv,
        w_enc_out,
    )
    blocks = ring_blocks(own_half + exchanged(away_half, CORE).astype(jnp.float32))
    current = own_of(0)
    last = micro_count + GROUPS - 2
    onward = [(s, s + GROUP) for s in range(SIZE - GROUP)]
    memories = []
    for step in range(last + 1):
        if step:
            slot = jnp.clip(step - group_index, 0, micro_count - 1)
            lengths = lax.dynamic_index_in_dim(doc_lengths, slot, 0, keepdims=False)
            pieces = ring_pieces(norm_rows(current, layer_gain).astype(jnp.bfloat16))
            if step == last:
                pieces, finished = lax.optimization_barrier((pieces, result_of_first))
                memories.append(spread(finished))
            doc, place = doc_there[:half], place_there[:half]
            allowed = (doc[:, None] == doc[None, :]) & live_rows(doc, place, lengths)[None, :]
            blocks = layer_terms(pieces, allowed, w_enc_qkv, maps_other, w_enc_out, out_other)
            if step == last:
                blocks, memories[-1] = lax.optimization_barrier((blocks, memories[-1]))
        summed = add_exchanged(reduce_ring(*blocks), lambda block: exchanged(block, PLANE))
        result = (current.astype(jnp.float32) + summed).astype(jnp.bfloat16)
        if step == last - 1:
            result_of_first = result
        if step == last:
            memories.append(spread(result))
        if step < last:
            current = lax.ppermute(result, "section", onward)
            if step + 1 < micro_count:
                current = jnp.where(group_index == 0, own_of(step + 1), current)
    memories = [gather_rows(rows) for rows in memories]

    index = jnp.arange(decoder_rows)
    query_doc = ring_y ^ (index // share % doc_count)
    query_place = (core ^ (index // (decoder_rows // 2))) * share + index % share
    query_order = query_doc * docid_span + query_place
    cross_same = query_doc[:, None] == doc_there[None, :]
    dec_normed = norm_rows(docid_embed, dec_gain[0]).astype(jnp.bfloat16)
    own_queries = jnp.dot(
        dec_normed.reshape(-1, model_width),
        cross_query_key_value_weight[0].T,
        preferred_element_type=jnp.float32,
    ).astype(jnp.bfloat16)
    own_queries = own_queries.reshape(micro_count, decoder_rows, -1, HD)

    mixtures = []
    for m in range(micro_count):
        heads = jnp.einsum(
            "rd,qcd->qrc",
            memories[m],
            cross_query_key_value_weight[1:],
            preferred_element_type=jnp.float32,
        ).astype(jnp.bfloat16)
        heads = heads.reshape(2, row_count, -1, HD)
        allowed = cross_same & live_rows(doc_there, place_there, doc_lengths[m])[None, :]
        queries = jnp.take(own_queries[m], query_order, axis=0)
        mixed = attend(queries, heads[0], heads[1], allowed)
        mixtures.append(mixed.reshape(decoder_rows // share, share, -1))
    cross_mixture = jnp.stack(mixtures, 1).reshape(micro_count * decoder_rows, -1)
    cross_sum = reduce_ring(*ring_blocks(reduce_core(cross_mixture, w_cross_out)))
    for partner in ((1, 0, 3, 2, 5, 4, 7, 6), (7, 2, 1, 4, 3, 6, 5, 0), (3, 6, 5, 0, 7, 2, 1, 4)):
        route = tuple(enumerate(partner))
        cross_sum = add_exchanged(cross_sum, lambda block, route=route: along_z(block, route))
    own_docid = lax.dynamic_slice_in_dim(
        docid_embed, ring_y * docid_span + core * share, share, 1
    ).reshape(micro_count * share, model_width)
    closing_own = norm_rows(own_docid.astype(jnp.float32) + cross_sum, dec_gain[1]).astype(
        jnp.bfloat16
    )
    closing = gather_rows(closing_own)

    scores_here = jnp.dot(closing, docid_head_weight, preferred_element_type=jnp.float32)
    vocab_local = docid_head_weight.shape[1]
    index = jnp.arange(micro_count * decoder_rows)
    micro, doc = index // decoder_rows, index // docid_span % doc_count
    half, row = index // share % 2, index % share
    source = (((half ^ core) * doc_count + (doc ^ ring_y)) * micro_count + micro) * share + row
    scores_vocab = jnp.take(scores_here, source, axis=0).reshape(
        micro_count, decoder_rows, vocab_local
    )
    vocab_start = section_index * vocab_local
    matches = docid_targets[..., None] == vocab_start + jnp.arange(vocab_local)
    sums = jnp.stack(
        [
            jnp.sum(jnp.exp(scores_vocab), axis=-1),
            jnp.sum(jnp.where(matches, scores_vocab, 0.0), axis=-1),
        ]
    ).reshape(1, -1)
    axes = ("section", "rep")
    planes = lax.axis_size("rep")
    size = SIZE * planes
    everything = lax.all_to_all(
        jnp.broadcast_to(sums[None], (size, *sums.shape)), axes, 0, 0, tiled=True
    )
    sums = jnp.sum(everything.reshape(SIZE, planes, -1), axis=0)
    exponent_total, picked = jnp.moveaxis(sums.reshape(planes, 2, -1), 1, 0)
    token_losses = jnp.log(exponent_total) - picked
    token_loss = lax.dynamic_index_in_dim(
        token_losses, lax.axis_index("rep"), 0, keepdims=False
    ).reshape(micro_count, decoder_rows)
    mean_loss = jnp.mean(token_losses)
    return (scores_vocab.astype(jnp.bfloat16), token_loss, mean_loss)


def solution(mesh):
    in_specs = (
        P("rep", None, None),
        P("rep", None),
        P("rep", None, None),
        P("rep", None),
        P(),
        P(),
        P(None, "section", None),
        P("section", None),
        P(None, "section", None),
        P("section", None),
        P(None, "section"),
    )
    out_specs = (P("rep", None, "section"), P("rep", None), P())
    return jax.shard_map(shards, mesh=mesh, in_specs=in_specs, out_specs=out_specs, check_vma=False)
```

```python
import jax
import jax.numpy as jnp
from jax import lax
from jax.experimental import pallas as pl
from jax.experimental.pallas import tpu as pltpu
from jax.sharding import PartitionSpec as P

HD = 64
GROUPS = 4


CORE, PLANE, GROUP = 1, 8, 16
RING = (2, 4, 6)
SIZE = 64
VMEM_LIMIT = 48 * 1024 * 1024


def exchanged(block, mask):
    return lax.ppermute(block, "section", [(s, s ^ mask) for s in range(SIZE)])


def norm_rows(values, gain):
    values = values.astype(jnp.float32)
    scale = lax.rsqrt(jnp.mean(values * values, axis=-1, keepdims=True) + 1e-06)
    return values * scale * gain


def attend(queries, key_rows, values, allowed):
    scores = jnp.einsum("qhe,khe->hqk", queries, key_rows, preferred_element_type=jnp.float32)
    weights = jnp.where(allowed[None], jnp.exp(scores), 0.0)
    probabilities = (weights / jnp.sum(weights, axis=-1, keepdims=True)).astype(jnp.bfloat16)
    mixture = jnp.einsum("hqk,khe->qhe", probabilities, values, preferred_element_type=jnp.float32)
    return mixture.astype(jnp.bfloat16)


def across(a, b):
    return lax.dot_general(a, b, (((1,), (1,)), ((), ())), preferred_element_type=jnp.float32)


def head_mixtures(projected, mask):
    mixtures = []
    for low in range(0, projected[0].shape[1], HD):
        queries, key_rows, values = (columns[:, low : low + HD] for columns in projected)
        weights = jnp.where(mask > 0.0, jnp.exp(across(queries, key_rows)), 0.0)
        probabilities = (weights / jnp.sum(weights, axis=-1, keepdims=True)).astype(jnp.bfloat16)
        mixtures.append(jnp.dot(probabilities, values, preferred_element_type=jnp.float32))
    return jnp.concatenate(mixtures, 1).astype(jnp.bfloat16)


def layer_kernel(first, second, third, fourth, mask, *refs):
    sources, outputs, held, sems = refs[:4], refs[4:8], refs[8:12], refs[12]
    size = first.shape[0]
    copies = []
    for array in (0, 1):
        for member in range(3):
            copies.append(
                pltpu.make_async_copy(
                    sources[array].at[member], held[array].at[member], sems.at[len(copies)]
                )
            )
    for array in (2, 3):
        copies.append(pltpu.make_async_copy(sources[array], held[array], sems.at[len(copies)]))
    for copy in copies:
        copy.start()
    rows = jnp.concatenate([piece[...] for piece in (first, second, third, fourth)], 0)
    projected = []
    for array in (0, 1):
        for member in range(3):
            copies[3 * array + member].wait()
        pj = across(rows, held[array][...].reshape(576, 4096)).astype(jnp.bfloat16)
        projected += [pj[:, :192], pj[:, 192:384], pj[:, 384:]]
    mixed = [head_mixtures(projected[3 * k : 3 * k + 3], mask[...]) for k in (0, 1)]
    copies[6].wait()
    copies[7].wait()
    total = jnp.dot(mixed[0], held[2][...], preferred_element_type=jnp.float32)
    total += jnp.dot(mixed[1], held[3][...], preferred_element_type=jnp.float32)
    for k, output in enumerate(outputs):
        output[...] = total[k * size : (k + 1) * size, :].astype(output.dtype)


def layer_terms(pieces, allowed, maps, maps_other, out, out_other):
    size, width = pieces[0].shape
    whole = pl.BlockSpec(memory_space=pltpu.VMEM)
    types = [jnp.float32] + [jnp.bfloat16] * 3
    return pl.pallas_call(
        layer_kernel,
        in_specs=[whole] * 5 + [pl.BlockSpec(memory_space=pl.ANY)] * 4,
        out_specs=[whole] * 4,
        out_shape=[jax.ShapeDtypeStruct((size, width), dtype) for dtype in types],
        scratch_shapes=[pltpu.VMEM(a.shape, a.dtype) for a in (maps, maps_other, out, out_other)]
        + [pltpu.SemaphoreType.DMA((8,))],
        compiler_params=pltpu.CompilerParams(vmem_limit_bytes=VMEM_LIMIT),
        cost_estimate=pl.CostEstimate(
            flops=16 * size * width * maps.shape[1] * 4,
            bytes_accessed=16 * maps.shape[1] * width,
            transcendentals=0,
        ),
    )(*pieces, allowed.astype(jnp.float32), maps, maps_other, out, out_other)


def first_kernel(place, gain, mask, documents, maps, out, own, away, held, maps_held, out_held, total, sems):
    copies = [
        pltpu.make_async_copy(documents.at[0], held, sems.at[0]),
        pltpu.make_async_copy(maps, maps_held, sems.at[1]),
        pltpu.make_async_copy(out, out_held, sems.at[2]),
    ]
    for copy in copies:
        copy.start()
    copies[0].wait()
    rows = norm_rows(held[...], gain[...]).astype(jnp.bfloat16)
    copies[1].wait()
    columns = maps_held.shape[1]
    projected = across(rows, maps_held[...].reshape(3 * columns, rows.shape[1]))
    projected = projected.astype(jnp.bfloat16)
    members = [projected[:, k * columns : (k + 1) * columns] for k in range(3)]
    mixed = head_mixtures(members, mask[...])
    copies[2].wait()
    total[...] = jnp.dot(mixed, out_held[...], preferred_element_type=jnp.float32)
    core, ring_y = place[0], place[1]
    half = own.shape[0]
    size = half // 4
    for k in range(4):
        there = (ring_y ^ k) * size
        here = pl.ds(pl.multiple_of(core * half + there, size), size)
        other = pl.ds(pl.multiple_of((1 - core) * half + there, size), size)
        own[k * size : (k + 1) * size, :] = total[here, :]
        away[k * size : (k + 1) * size, :] = total[other, :].astype(away.dtype)


def first_terms(place, gain, allowed, documents, maps, out):
    _, count, width = documents.shape
    whole = pl.BlockSpec(memory_space=pltpu.VMEM)
    large = pl.BlockSpec(memory_space=pl.ANY)
    return pl.pallas_call(
        first_kernel,
        in_specs=[pl.BlockSpec(memory_space=pltpu.SMEM), whole, whole, large, large, large],
        out_specs=[whole, whole],
        out_shape=[
            jax.ShapeDtypeStruct((count // 2, width), jnp.float32),
            jax.ShapeDtypeStruct((count // 2, width), jnp.bfloat16),
        ],
        scratch_shapes=[
            pltpu.VMEM((count, width), documents.dtype),
            pltpu.VMEM(maps.shape, maps.dtype),
            pltpu.VMEM(out.shape, out.dtype),
            pltpu.VMEM((count, width), jnp.float32),
            pltpu.SemaphoreType.DMA((3,)),
        ],
        compiler_params=pltpu.CompilerParams(vmem_limit_bytes=VMEM_LIMIT),
        cost_estimate=pl.CostEstimate(
            flops=8 * count * width * maps.shape[1],
            bytes_accessed=8 * maps.shape[1] * width,
            transcendentals=0,
        ),
    )(place, gain, allowed.astype(jnp.float32), documents, maps, out)


def ring_pieces(own):
    return [own] + [exchanged(own, mask) for mask in RING]


def gather_rows(own):
    ring = jnp.concatenate(ring_pieces(own), 0)
    return jnp.concatenate([ring, exchanged(ring, CORE)], 0)


def along_z(block, route):
    pairs = [(z * PLANE + s, to * PLANE + s) for z, to in route for s in range(PLANE)]
    return lax.ppermute(block, "section", pairs)


def reduce_core(mixture, weight):
    half = mixture.shape[0] // 2
    away = jnp.dot(mixture[half:], weight, preferred_element_type=jnp.float32)
    arrived = exchanged(away.astype(jnp.bfloat16), CORE)
    own = jnp.dot(mixture[:half], weight, preferred_element_type=jnp.float32)
    return own + arrived.astype(jnp.float32)


def ring_blocks(ring):
    rows = ring.shape[0] // 4
    sent = ring.astype(jnp.bfloat16)
    return [ring[:rows]] + [sent[k * rows : (k + 1) * rows] for k in range(1, 4)]


def reduce_ring(total, *blocks):
    for mask, block in zip(RING, blocks):
        total = total + exchanged(block, mask).astype(jnp.float32)
    return total


def add_exchanged(total, exchange):
    return total + exchange(total.astype(jnp.bfloat16)).astype(jnp.float32)


def shards(
    document_token_embedding,
    doc_lengths,
    docid_embed,
    docid_targets,
    enc_gain,
    dec_gain,
    w_enc_qkv,
    w_enc_out,
    cross_query_key_value_weight,
    w_cross_out,
    docid_head_weight,
):
    section_index = lax.axis_index("section")
    core = section_index % 2
    ring_y = section_index // 2 % 4
    depth = section_index // PLANE
    group_index = section_index // GROUP
    micro_count, row_count, model_width = document_token_embedding.shape
    doc_count = doc_lengths.shape[1]
    doc_span = row_count // doc_count
    decoder_rows = docid_embed.shape[1]
    docid_span = decoder_rows // doc_count
    block_rows = doc_span // 2
    share = docid_span // 2

    index = jnp.arange(row_count)
    source_block = (core ^ (index // (row_count // 2))) * 4 + (ring_y ^ (index // block_rows % 4))
    order_there = source_block * block_rows + index % block_rows
    doc_there, place_there = order_there // doc_span, order_there % doc_span
    doc_plain, place_plain = index // doc_span, index % doc_span

    def live_rows(doc, place, lengths):
        owner = doc[:, None] == jnp.arange(doc_count)
        return place < jnp.sum(jnp.where(owner, lengths[None, :], 0), axis=1)

    maps_other = exchanged(w_enc_qkv, CORE)
    out_other = exchanged(w_enc_out, CORE)
    half = row_count // 2

    own_start = (core * 4 + ring_y) * block_rows

    def own_of(m):
        return lax.dynamic_slice_in_dim(document_token_embedding[m], own_start, block_rows, 0)

    def relayed(own, up, down):
        arrived = along_z(own, (up, down))
        return jnp.where((depth == up[1]) | (depth == down[1]), arrived, own)

    def spread(finished):
        own = norm_rows(finished, enc_gain[GROUPS]).astype(jnp.bfloat16)
        arrived = [along_z(own, ((7, to), (6, 5 - to))) for to in range(3)]
        for to in range(3):
            own = jnp.where((depth == to) | (depth == 5 - to), arrived[to], own)
        return own

    layer_gain = lax.dynamic_index_in_dim(enc_gain, group_index, 0, keepdims=False)
    allowed = doc_plain[:, None] == doc_plain[None, :]
    allowed = allowed & live_rows(doc_plain, place_plain, doc_lengths[0])[None, :]
    own_half, away_half = first_terms(
        jnp.stack([core, ring_y]).astype(jnp.int32),
        enc_gain[:1],
        allowed,
        document_token_embedding,
        w_enc_qkv,
        w_enc_out,
    )
    blocks = ring_blocks(own_half + exchanged(away_half, CORE).astype(jnp.float32))
    current = own_of(0)
    last = micro_count + GROUPS - 2
    onward = [(s, s + GROUP) for s in range(SIZE - GROUP)]
    memories = []
    for step in range(last + 1):
        if step:
            slot = jnp.clip(step - group_index, 0, micro_count - 1)
            lengths = lax.dynamic_index_in_dim(doc_lengths, slot, 0, keepdims=False)
            pieces = ring_pieces(norm_rows(current, layer_gain).astype(jnp.bfloat16))
            if step == last:
                pieces, first_result = lax.optimization_barrier((pieces, first_result))
                first_memory = norm_rows(first_result, enc_gain[GROUPS]).astype(jnp.bfloat16)
                first_memory = relayed(first_memory, (7, 0), (6, 5))
            doc, place = doc_there[:half], place_there[:half]
            allowed = (doc[:, None] == doc[None, :]) & live_rows(doc, place, lengths)[None, :]
            blocks = layer_terms(pieces, allowed, w_enc_qkv, maps_other, w_enc_out, out_other)
        if step == last:
            blocks, first_memory = lax.optimization_barrier((blocks, first_memory))
            first_memory = relayed(first_memory, (0, 1), (5, 4))
            first_memory = relayed(first_memory, (1, 2), (4, 3))
        summed = reduce_ring(*blocks)
        if step == last:
            summed, first_memory = lax.optimization_barrier((summed, first_memory))
            memories.append(first_memory)
        summed = add_exchanged(summed, lambda block: exchanged(block, PLANE))
        result = (current.astype(jnp.float32) + summed).astype(jnp.bfloat16)
        if step == last - 1:
            first_result = result
        if step == last:
            memories.append(spread(result))
        if step < last:
            current = lax.ppermute(result, "section", onward)
            if step + 1 < micro_count:
                current = jnp.where(group_index == 0, own_of(step + 1), current)
    memories = [gather_rows(rows) for rows in memories]

    index = jnp.arange(decoder_rows)
    query_doc = ring_y ^ (index // share % doc_count)
    query_place = (core ^ (index // (decoder_rows // 2))) * share + index % share
    query_order = query_doc * docid_span + query_place
    cross_same = query_doc[:, None] == doc_there[None, :]
    dec_normed = norm_rows(docid_embed, dec_gain[0]).astype(jnp.bfloat16)
    own_queries = jnp.dot(
        dec_normed.reshape(-1, model_width),
        cross_query_key_value_weight[0].T,
        preferred_element_type=jnp.float32,
    ).astype(jnp.bfloat16)
    own_queries = own_queries.reshape(micro_count, decoder_rows, -1, HD)

    mixtures = []
    for m in range(micro_count):
        heads = jnp.einsum(
            "rd,qcd->qrc",
            memories[m],
            cross_query_key_value_weight[1:],
            preferred_element_type=jnp.float32,
        ).astype(jnp.bfloat16)
        heads = heads.reshape(2, row_count, -1, HD)
        allowed = cross_same & live_rows(doc_there, place_there, doc_lengths[m])[None, :]
        queries = jnp.take(own_queries[m], query_order, axis=0)
        mixed = attend(queries, heads[0], heads[1], allowed)
        mixtures.append(mixed.reshape(decoder_rows // share, share, -1))
    cross_mixture = jnp.stack(mixtures, 1).reshape(micro_count * decoder_rows, -1)
    cross_sum = reduce_ring(*ring_blocks(reduce_core(cross_mixture, w_cross_out)))
    for partner in ((1, 0, 3, 2, 5, 4, 7, 6), (7, 2, 1, 4, 3, 6, 5, 0), (3, 6, 5, 0, 7, 2, 1, 4)):
        route = tuple(enumerate(partner))
        cross_sum = add_exchanged(cross_sum, lambda block, route=route: along_z(block, route))
    own_docid = lax.dynamic_slice_in_dim(
        docid_embed, ring_y * docid_span + core * share, share, 1
    ).reshape(micro_count * share, model_width)
    closing_own = norm_rows(own_docid.astype(jnp.float32) + cross_sum, dec_gain[1]).astype(
        jnp.bfloat16
    )
    closing = gather_rows(closing_own)

    scores_here = jnp.dot(closing, docid_head_weight, preferred_element_type=jnp.float32)
    vocab_local = docid_head_weight.shape[1]
    index = jnp.arange(micro_count * decoder_rows)
    micro, doc = index // decoder_rows, index // docid_span % doc_count
    half, row = index // share % 2, index % share
    source = (((half ^ core) * doc_count + (doc ^ ring_y)) * micro_count + micro) * share + row
    scores_vocab = jnp.take(scores_here, source, axis=0).reshape(
        micro_count, decoder_rows, vocab_local
    )
    vocab_start = section_index * vocab_local
    matches = docid_targets[..., None] == vocab_start + jnp.arange(vocab_local)
    sums = jnp.stack(
        [
            jnp.sum(jnp.exp(scores_vocab), axis=-1),
            jnp.sum(jnp.where(matches, scores_vocab, 0.0), axis=-1),
        ]
    ).reshape(1, -1)
    axes = ("section", "rep")
    planes = lax.axis_size("rep")
    size = SIZE * planes
    everything = lax.all_to_all(
        jnp.broadcast_to(sums, (size, sums.shape[1])), axes, 0, 0, tiled=True
    )
    sums = jnp.sum(everything.reshape(SIZE, planes, -1), axis=0)
    exponent_total, picked = jnp.moveaxis(sums.reshape(planes, 2, -1), 1, 0)
    token_losses = jnp.log(exponent_total) - picked
    token_loss = lax.dynamic_index_in_dim(
        token_losses, lax.axis_index("rep"), 0, keepdims=False
    ).reshape(micro_count, decoder_rows)
    mean_loss = jnp.mean(token_losses)
    return (scores_vocab.astype(jnp.bfloat16), token_loss, mean_loss)


def solution(mesh):
    in_specs = (
        P("rep", None, None),
        P("rep", None),
        P("rep", None, None),
        P("rep", None),
        P(),
        P(),
        P(None, "section", None),
        P("section", None),
        P(None, "section", None),
        P("section", None),
        P(None, "section"),
    )
    out_specs = (P("rep", None, "section"), P("rep", None), P())
    return jax.shard_map(shards, mesh=mesh, in_specs=in_specs, out_specs=out_specs, check_vma=False)
```

```python
import jax
import jax.numpy as jnp
from jax import lax
from jax.experimental import pallas as pl
from jax.experimental.pallas import tpu as pltpu
from jax.sharding import PartitionSpec as P

HD = 64
GROUPS = 4


CORE, PLANE, GROUP = 1, 8, 16
RING = (2, 4, 6)
FAR_FIRST = (4, 2, 6)
SIZE = 64
VMEM_LIMIT = 48 * 1024 * 1024
FIRST_LIMIT = 61 * 1024 * 1024


def exchanged(block, mask):
    return lax.ppermute(block, "section", [(s, s ^ mask) for s in range(SIZE)])


def norm_rows(values, gain):
    values = values.astype(jnp.float32)
    scale = lax.rsqrt(jnp.mean(values * values, axis=-1, keepdims=True) + 1e-06)
    return values * scale * gain


def attend(queries, key_rows, values, allowed):
    scores = jnp.einsum("qhe,khe->hqk", queries, key_rows, preferred_element_type=jnp.float32)
    weights = jnp.where(allowed[None], jnp.exp(scores), 0.0)
    probabilities = (weights / jnp.sum(weights, axis=-1, keepdims=True)).astype(jnp.bfloat16)
    mixture = jnp.einsum("hqk,khe->qhe", probabilities, values, preferred_element_type=jnp.float32)
    return mixture.astype(jnp.bfloat16)


def across(a, b):
    return lax.dot_general(a, b, (((1,), (1,)), ((), ())), preferred_element_type=jnp.float32)


def head_mixtures(projected, mask):
    mixtures = []
    for low in range(0, projected[0].shape[1], HD):
        queries, key_rows, values = (columns[:, low : low + HD] for columns in projected)
        weights = jnp.where(mask > 0.0, jnp.exp(across(queries, key_rows)), 0.0)
        probabilities = (weights / jnp.sum(weights, axis=-1, keepdims=True)).astype(jnp.bfloat16)
        mixtures.append(jnp.dot(probabilities, values, preferred_element_type=jnp.float32))
    return jnp.concatenate(mixtures, 1).astype(jnp.bfloat16)


def layer_kernel(first, second, third, fourth, mask, *refs):
    sources, outputs, held, sems = refs[:4], refs[4:8], refs[8:12], refs[12]
    size = first.shape[0]
    copies = []
    for array in (0, 1):
        for member in range(3):
            copies.append(
                pltpu.make_async_copy(
                    sources[array].at[member], held[array].at[member], sems.at[len(copies)]
                )
            )
    for array in (2, 3):
        copies.append(pltpu.make_async_copy(sources[array], held[array], sems.at[len(copies)]))
    for copy in copies:
        copy.start()
    rows = jnp.concatenate([piece[...] for piece in (first, second, third, fourth)], 0)
    projected = []
    for array in (0, 1):
        for member in range(3):
            copies[3 * array + member].wait()
        pj = across(rows, held[array][...].reshape(576, 4096)).astype(jnp.bfloat16)
        projected += [pj[:, :192], pj[:, 192:384], pj[:, 384:]]
    mixed = [head_mixtures(projected[3 * k : 3 * k + 3], mask[...]) for k in (0, 1)]
    copies[6].wait()
    copies[7].wait()
    total = jnp.dot(mixed[0], held[2][...], preferred_element_type=jnp.float32)
    total += jnp.dot(mixed[1], held[3][...], preferred_element_type=jnp.float32)
    for k, output in enumerate(outputs):
        output[...] = total[k * size : (k + 1) * size, :].astype(output.dtype)


def layer_terms(pieces, allowed, maps, maps_other, out, out_other):
    size, width = pieces[0].shape
    whole = pl.BlockSpec(memory_space=pltpu.VMEM)
    types = [jnp.float32] + [jnp.bfloat16] * 3
    return pl.pallas_call(
        layer_kernel,
        in_specs=[whole] * 5 + [pl.BlockSpec(memory_space=pl.ANY)] * 4,
        out_specs=[whole] * 4,
        out_shape=[jax.ShapeDtypeStruct((size, width), dtype) for dtype in types],
        scratch_shapes=[pltpu.VMEM(a.shape, a.dtype) for a in (maps, maps_other, out, out_other)]
        + [pltpu.SemaphoreType.DMA((8,))],
        compiler_params=pltpu.CompilerParams(vmem_limit_bytes=VMEM_LIMIT),
        cost_estimate=pl.CostEstimate(
            flops=16 * size * width * maps.shape[1] * 4,
            bytes_accessed=16 * maps.shape[1] * width,
            transcendentals=0,
        ),
    )(*pieces, allowed.astype(jnp.float32), maps, maps_other, out, out_other)


def first_kernel(place, lengths, gains, documents, maps, out, own, away, held, maps_held, out_held, total, sems):
    copies = [
        pltpu.make_async_copy(documents.at[0], held, sems.at[0]),
        pltpu.make_async_copy(maps, maps_held, sems.at[1]),
        pltpu.make_async_copy(out, out_held, sems.at[2]),
    ]
    for copy in copies:
        copy.start()
    copies[0].wait()
    rows = norm_rows(held[...], gains[0:1, :]).astype(jnp.bfloat16)
    count, doc_count = rows.shape[0], lengths.shape[1]
    span = count // doc_count
    row_doc = lax.div(lax.broadcasted_iota(jnp.int32, (count, count), 0), span)
    column = lax.broadcasted_iota(jnp.int32, (count, count), 1)
    mask = jnp.zeros((count, count), jnp.float32)
    for doc in range(doc_count):
        live = (column >= doc * span) & (column < doc * span + lengths[0, doc])
        mask = jnp.where(live & (row_doc == doc), 1.0, mask)
    copies[1].wait()
    columns = maps_held.shape[1]
    projected = across(rows, maps_held[...].reshape(3 * columns, rows.shape[1]))
    projected = projected.astype(jnp.bfloat16)
    members = [projected[:, k * columns : (k + 1) * columns] for k in range(3)]
    mixed = head_mixtures(members, mask)
    copies[2].wait()
    total[...] = jnp.dot(mixed, out_held[...], preferred_element_type=jnp.float32)
    core, ring_y = place[0], place[1]
    half = own.shape[0]
    size = half // 4
    for k in range(4):
        there = (ring_y ^ k) * size
        here = pl.ds(pl.multiple_of(core * half + there, size), size)
        other = pl.ds(pl.multiple_of((1 - core) * half + there, size), size)
        own[k * size : (k + 1) * size, :] = total[here, :]
        away[k * size : (k + 1) * size, :] = total[other, :].astype(away.dtype)


def first_terms(place, lengths, gains, documents, maps, out):
    _, count, width = documents.shape
    whole = pl.BlockSpec(memory_space=pltpu.VMEM)
    large = pl.BlockSpec(memory_space=pl.ANY)
    return pl.pallas_call(
        first_kernel,
        in_specs=[pl.BlockSpec(memory_space=pltpu.SMEM)] * 2 + [whole, large, large, large],
        out_specs=[whole, whole],
        out_shape=[
            jax.ShapeDtypeStruct((count // 2, width), jnp.float32),
            jax.ShapeDtypeStruct((count // 2, width), jnp.bfloat16),
        ],
        scratch_shapes=[
            pltpu.VMEM((count, width), documents.dtype),
            pltpu.VMEM(maps.shape, maps.dtype),
            pltpu.VMEM(out.shape, out.dtype),
            pltpu.VMEM((count, width), jnp.float32),
            pltpu.SemaphoreType.DMA((3,)),
        ],
        compiler_params=pltpu.CompilerParams(vmem_limit_bytes=FIRST_LIMIT),
        cost_estimate=pl.CostEstimate(
            flops=8 * count * width * maps.shape[1],
            bytes_accessed=8 * maps.shape[1] * width,
            transcendentals=0,
        ),
    )(place, lengths, gains, documents, maps, out)


def ring_pieces(own):
    pieces = {mask: exchanged(own, mask) for mask in FAR_FIRST}
    return [own] + [pieces[mask] for mask in RING]


def gather_rows(own):
    ring = jnp.concatenate(ring_pieces(own), 0)
    return jnp.concatenate([ring, exchanged(ring, CORE)], 0)


def along_z(block, route):
    pairs = [(z * PLANE + s, to * PLANE + s) for z, to in route for s in range(PLANE)]
    return lax.ppermute(block, "section", pairs)


def reduce_core(mixture, weight):
    half = mixture.shape[0] // 2
    away = jnp.dot(mixture[half:], weight, preferred_element_type=jnp.float32)
    arrived = exchanged(away.astype(jnp.bfloat16), CORE)
    own = jnp.dot(mixture[:half], weight, preferred_element_type=jnp.float32)
    return own + arrived.astype(jnp.float32)


def ring_blocks(ring):
    rows = ring.shape[0] // 4
    sent = ring.astype(jnp.bfloat16)
    return [ring[:rows]] + [sent[k * rows : (k + 1) * rows] for k in range(1, 4)]


def reduce_ring(total, *blocks):
    arrived = {mask: exchanged(blocks[mask // 2 - 1], mask) for mask in FAR_FIRST}
    for mask in RING:
        total = total + arrived[mask].astype(jnp.float32)
    return total


def add_exchanged(total, exchange):
    return total + exchange(total.astype(jnp.bfloat16)).astype(jnp.float32)


def shards(
    document_token_embedding,
    doc_lengths,
    docid_embed,
    docid_targets,
    enc_gain,
    dec_gain,
    w_enc_qkv,
    w_enc_out,
    cross_query_key_value_weight,
    w_cross_out,
    docid_head_weight,
):
    section_index = lax.axis_index("section")
    core = section_index % 2
    ring_y = section_index // 2 % 4
    depth = section_index // PLANE
    group_index = section_index // GROUP
    micro_count, row_count, model_width = document_token_embedding.shape
    doc_count = doc_lengths.shape[1]
    doc_span = row_count // doc_count
    decoder_rows = docid_embed.shape[1]
    docid_span = decoder_rows // doc_count
    block_rows = doc_span // 2
    share = docid_span // 2

    index = jnp.arange(row_count)
    source_block = (core ^ (index // (row_count // 2))) * 4 + (ring_y ^ (index // block_rows % 4))
    order_there = source_block * block_rows + index % block_rows
    doc_there, place_there = order_there // doc_span, order_there % doc_span

    def live_rows(doc, place, lengths):
        owner = doc[:, None] == jnp.arange(doc_count)
        return place < jnp.sum(jnp.where(owner, lengths[None, :], 0), axis=1)

    maps_other = exchanged(w_enc_qkv, CORE)
    out_other = exchanged(w_enc_out, CORE)
    half = row_count // 2

    own_start = (core * 4 + ring_y) * block_rows

    def own_of(m):
        return lax.dynamic_slice_in_dim(document_token_embedding[m], own_start, block_rows, 0)

    def spread(finished):
        own = norm_rows(finished, enc_gain[GROUPS]).astype(jnp.bfloat16)
        arrived = [along_z(own, ((7, to), (6, 5 - to))) for to in range(3)]
        for to in range(3):
            own = jnp.where((depth == to) | (depth == 5 - to), arrived[to], own)
        return own

    layer_gain = lax.dynamic_index_in_dim(enc_gain, group_index, 0, keepdims=False)
    own_half, away_half = first_terms(
        jnp.stack([core, ring_y]).astype(jnp.int32),
        doc_lengths,
        enc_gain,
        document_token_embedding,
        w_enc_qkv,
        w_enc_out,
    )
    blocks = ring_blocks(own_half + exchanged(away_half, CORE).astype(jnp.float32))
    current = own_of(0)
    last = micro_count + GROUPS - 2
    onward = [(s, s + GROUP) for s in range(SIZE - GROUP)]
    memories = []
    for step in range(last + 1):
        if step:
            slot = jnp.clip(step - group_index, 0, micro_count - 1)
            lengths = lax.dynamic_index_in_dim(doc_lengths, slot, 0, keepdims=False)
            pieces = ring_pieces(norm_rows(current, layer_gain).astype(jnp.bfloat16))
            if step == last:
                pieces, finished = lax.optimization_barrier((pieces, result_of_first))
                memories.append(spread(finished))
            doc, place = doc_there[:half], place_there[:half]
            allowed = (doc[:, None] == doc[None, :]) & live_rows(doc, place, lengths)[None, :]
            blocks = layer_terms(pieces, allowed, w_enc_qkv, maps_other, w_enc_out, out_other)
            if step == last:
                blocks, memories[-1] = lax.optimization_barrier((blocks, memories[-1]))
        summed = add_exchanged(reduce_ring(*blocks), lambda block: exchanged(block, PLANE))
        result = (current.astype(jnp.float32) + summed).astype(jnp.bfloat16)
        if step == last - 1:
            result_of_first = result
        if step == last:
            memories.append(spread(result))
        if step < last:
            current = lax.ppermute(result, "section", onward)
            if step + 1 < micro_count:
                current = jnp.where(group_index == 0, own_of(step + 1), current)
    memories = [gather_rows(rows) for rows in memories]

    index = jnp.arange(decoder_rows)
    query_doc = ring_y ^ (index // share % doc_count)
    query_place = (core ^ (index // (decoder_rows // 2))) * share + index % share
    query_order = query_doc * docid_span + query_place
    cross_same = query_doc[:, None] == doc_there[None, :]
    dec_normed = norm_rows(docid_embed, dec_gain[0]).astype(jnp.bfloat16)
    own_queries = jnp.dot(
        dec_normed.reshape(-1, model_width),
        cross_query_key_value_weight[0].T,
        preferred_element_type=jnp.float32,
    ).astype(jnp.bfloat16)
    own_queries = own_queries.reshape(micro_count, decoder_rows, -1, HD)

    mixtures = []
    for m in range(micro_count):
        heads = jnp.einsum(
            "rd,qcd->qrc",
            memories[m],
            cross_query_key_value_weight[1:],
            preferred_element_type=jnp.float32,
        ).astype(jnp.bfloat16)
        heads = heads.reshape(2, row_count, -1, HD)
        allowed = cross_same & live_rows(doc_there, place_there, doc_lengths[m])[None, :]
        queries = jnp.take(own_queries[m], query_order, axis=0)
        mixed = attend(queries, heads[0], heads[1], allowed)
        mixtures.append(mixed.reshape(decoder_rows // share, share, -1))
    cross_mixture = jnp.stack(mixtures, 1).reshape(micro_count * decoder_rows, -1)
    cross_sum = reduce_ring(*ring_blocks(reduce_core(cross_mixture, w_cross_out)))
    for partner in ((1, 0, 3, 2, 5, 4, 7, 6), (7, 2, 1, 4, 3, 6, 5, 0), (3, 6, 5, 0, 7, 2, 1, 4)):
        route = tuple(enumerate(partner))
        cross_sum = add_exchanged(cross_sum, lambda block, route=route: along_z(block, route))
    own_docid = lax.dynamic_slice_in_dim(
        docid_embed, ring_y * docid_span + core * share, share, 1
    ).reshape(micro_count * share, model_width)
    closing_own = norm_rows(own_docid.astype(jnp.float32) + cross_sum, dec_gain[1]).astype(
        jnp.bfloat16
    )
    closing = gather_rows(closing_own)

    scores_here = jnp.dot(closing, docid_head_weight, preferred_element_type=jnp.float32)
    vocab_local = docid_head_weight.shape[1]
    index = jnp.arange(micro_count * decoder_rows)
    micro, doc = index // decoder_rows, index // docid_span % doc_count
    half, row = index // share % 2, index % share
    source = (((half ^ core) * doc_count + (doc ^ ring_y)) * micro_count + micro) * share + row
    scores_vocab = jnp.take(scores_here, source, axis=0).reshape(
        micro_count, decoder_rows, vocab_local
    )
    vocab_start = section_index * vocab_local
    matches = docid_targets[..., None] == vocab_start + jnp.arange(vocab_local)
    sums = jnp.stack(
        [
            jnp.sum(jnp.exp(scores_vocab), axis=-1),
            jnp.sum(jnp.where(matches, scores_vocab, 0.0), axis=-1),
        ]
    ).reshape(1, -1)
    axes = ("section", "rep")
    planes = lax.axis_size("rep")
    size = SIZE * planes
    everything = lax.all_to_all(
        jnp.broadcast_to(sums[None], (size, *sums.shape)), axes, 0, 0, tiled=True
    )
    sums = jnp.sum(everything.reshape(SIZE, planes, -1), axis=0)
    exponent_total, picked = jnp.moveaxis(sums.reshape(planes, 2, -1), 1, 0)
    token_losses = jnp.log(exponent_total) - picked
    token_loss = lax.dynamic_index_in_dim(
        token_losses, lax.axis_index("rep"), 0, keepdims=False
    ).reshape(micro_count, decoder_rows)
    mean_loss = jnp.mean(token_losses)
    return (scores_vocab.astype(jnp.bfloat16), token_loss, mean_loss)


def solution(mesh):
    in_specs = (
        P("rep", None, None),
        P("rep", None),
        P("rep", None, None),
        P("rep", None),
        P(),
        P(),
        P(None, "section", None),
        P("section", None),
        P(None, "section", None),
        P("section", None),
        P(None, "section"),
    )
    out_specs = (P("rep", None, "section"), P("rep", None), P())
    return jax.shard_map(shards, mesh=mesh, in_specs=in_specs, out_specs=out_specs, check_vma=False)
```

```python
import jax
import jax.numpy as jnp
from jax import lax
from jax.experimental import pallas as pl
from jax.experimental.pallas import tpu as pltpu
from jax.sharding import PartitionSpec as P

HD = 64
GROUPS = 4


CORE, PLANE, GROUP = 1, 8, 16
RING = (2, 4, 6)
SIZE = 64
VMEM_LIMIT = 48 * 1024 * 1024
FIRST_LIMIT = 61 * 1024 * 1024


def exchanged(block, mask):
    return lax.ppermute(block, "section", [(s, s ^ mask) for s in range(SIZE)])


def norm_rows(values, gain):
    values = values.astype(jnp.float32)
    scale = lax.rsqrt(jnp.mean(values * values, axis=-1, keepdims=True) + 1e-06)
    return values * scale * gain


def attend(queries, key_rows, values, allowed):
    scores = jnp.einsum("qhe,khe->hqk", queries, key_rows, preferred_element_type=jnp.float32)
    weights = jnp.where(allowed[None], jnp.exp(scores), 0.0)
    probabilities = (weights / jnp.sum(weights, axis=-1, keepdims=True)).astype(jnp.bfloat16)
    mixture = jnp.einsum("hqk,khe->qhe", probabilities, values, preferred_element_type=jnp.float32)
    return mixture.astype(jnp.bfloat16)


def across(a, b):
    return lax.dot_general(a, b, (((1,), (1,)), ((), ())), preferred_element_type=jnp.float32)


def head_mixtures(projected, mask):
    mixtures = []
    for low in range(0, projected[0].shape[1], HD):
        queries, key_rows, values = (columns[:, low : low + HD] for columns in projected)
        weights = jnp.where(mask > 0.0, jnp.exp(across(queries, key_rows)), 0.0)
        probabilities = (weights / jnp.sum(weights, axis=-1, keepdims=True)).astype(jnp.bfloat16)
        mixtures.append(jnp.dot(probabilities, values, preferred_element_type=jnp.float32))
    return jnp.concatenate(mixtures, 1).astype(jnp.bfloat16)


def layer_kernel(first, second, third, fourth, mask, *refs):
    sources, outputs, held, sems = refs[:4], refs[4:8], refs[8:12], refs[12]
    size = first.shape[0]
    copies = []
    for array in (0, 1):
        for member in range(3):
            copies.append(
                pltpu.make_async_copy(
                    sources[array].at[member], held[array].at[member], sems.at[len(copies)]
                )
            )
    for array in (2, 3):
        copies.append(pltpu.make_async_copy(sources[array], held[array], sems.at[len(copies)]))
    for copy in copies:
        copy.start()
    rows = jnp.concatenate([piece[...] for piece in (first, second, third, fourth)], 0)
    projected = []
    for array in (0, 1):
        for member in range(3):
            copies[3 * array + member].wait()
        pj = across(rows, held[array][...].reshape(576, 4096)).astype(jnp.bfloat16)
        projected += [pj[:, :192], pj[:, 192:384], pj[:, 384:]]
    mixed = [head_mixtures(projected[3 * k : 3 * k + 3], mask[...]) for k in (0, 1)]
    copies[6].wait()
    copies[7].wait()
    total = jnp.dot(mixed[0], held[2][...], preferred_element_type=jnp.float32)
    total += jnp.dot(mixed[1], held[3][...], preferred_element_type=jnp.float32)
    for k, output in enumerate(outputs):
        output[...] = total[k * size : (k + 1) * size, :].astype(output.dtype)


def layer_terms(pieces, allowed, maps, maps_other, out, out_other):
    size, width = pieces[0].shape
    whole = pl.BlockSpec(memory_space=pltpu.VMEM)
    types = [jnp.float32] + [jnp.bfloat16] * 3
    return pl.pallas_call(
        layer_kernel,
        in_specs=[whole] * 5 + [pl.BlockSpec(memory_space=pl.ANY)] * 4,
        out_specs=[whole] * 4,
        out_shape=[jax.ShapeDtypeStruct((size, width), dtype) for dtype in types],
        scratch_shapes=[pltpu.VMEM(a.shape, a.dtype) for a in (maps, maps_other, out, out_other)]
        + [pltpu.SemaphoreType.DMA((8,))],
        compiler_params=pltpu.CompilerParams(vmem_limit_bytes=VMEM_LIMIT),
        cost_estimate=pl.CostEstimate(
            flops=16 * size * width * maps.shape[1] * 4,
            bytes_accessed=16 * maps.shape[1] * width,
            transcendentals=0,
        ),
    )(*pieces, allowed.astype(jnp.float32), maps, maps_other, out, out_other)


def first_kernel(place, lengths, gains, documents, maps, out, own, away, held, maps_held, out_held, total, sems):
    copies = [
        pltpu.make_async_copy(documents.at[0], held, sems.at[0]),
        pltpu.make_async_copy(maps, maps_held, sems.at[1]),
        pltpu.make_async_copy(out, out_held, sems.at[2]),
    ]
    for copy in copies:
        copy.start()
    copies[0].wait()
    rows = norm_rows(held[...], gains[0:1, :]).astype(jnp.bfloat16)
    count, doc_count = rows.shape[0], lengths.shape[1]
    span = count // doc_count
    row_doc = lax.div(lax.broadcasted_iota(jnp.int32, (count, count), 0), span)
    column = lax.broadcasted_iota(jnp.int32, (count, count), 1)
    mask = jnp.zeros((count, count), jnp.float32)
    for doc in range(doc_count):
        live = (column >= doc * span) & (column < doc * span + lengths[0, doc])
        mask = jnp.where(live & (row_doc == doc), 1.0, mask)
    copies[1].wait()
    columns = maps_held.shape[1]
    projected = across(rows, maps_held[...].reshape(3 * columns, rows.shape[1]))
    projected = projected.astype(jnp.bfloat16)
    members = [projected[:, k * columns : (k + 1) * columns] for k in range(3)]
    mixed = head_mixtures(members, mask)
    copies[2].wait()
    total[...] = jnp.dot(mixed, out_held[...], preferred_element_type=jnp.float32)
    core, ring_y = place[0], place[1]
    half = own.shape[0]
    size = half // 4
    for k in range(4):
        there = (ring_y ^ k) * size
        here = pl.ds(pl.multiple_of(core * half + there, size), size)
        other = pl.ds(pl.multiple_of((1 - core) * half + there, size), size)
        own[k * size : (k + 1) * size, :] = total[here, :]
        away[k * size : (k + 1) * size, :] = total[other, :].astype(away.dtype)


def first_terms(place, lengths, gains, documents, maps, out):
    _, count, width = documents.shape
    whole = pl.BlockSpec(memory_space=pltpu.VMEM)
    large = pl.BlockSpec(memory_space=pl.ANY)
    return pl.pallas_call(
        first_kernel,
        in_specs=[pl.BlockSpec(memory_space=pltpu.SMEM)] * 2 + [whole, large, large, large],
        out_specs=[whole, whole],
        out_shape=[
            jax.ShapeDtypeStruct((count // 2, width), jnp.float32),
            jax.ShapeDtypeStruct((count // 2, width), jnp.bfloat16),
        ],
        scratch_shapes=[
            pltpu.VMEM((count, width), documents.dtype),
            pltpu.VMEM(maps.shape, maps.dtype),
            pltpu.VMEM(out.shape, out.dtype),
            pltpu.VMEM((count, width), jnp.float32),
            pltpu.SemaphoreType.DMA((3,)),
        ],
        compiler_params=pltpu.CompilerParams(vmem_limit_bytes=FIRST_LIMIT),
        cost_estimate=pl.CostEstimate(
            flops=8 * count * width * maps.shape[1],
            bytes_accessed=8 * maps.shape[1] * width,
            transcendentals=0,
        ),
    )(place, lengths, gains, documents, maps, out)


def ring_pieces(own):
    pieces = {mask: exchanged(own, mask) for mask in RING}
    return [own] + [pieces[mask] for mask in RING]


def gather_rows(own):
    ring = jnp.concatenate(ring_pieces(own), 0)
    return jnp.concatenate([ring, exchanged(ring, CORE)], 0)


def along_z(block, route):
    pairs = [(z * PLANE + s, to * PLANE + s) for z, to in route for s in range(PLANE)]
    return lax.ppermute(block, "section", pairs)


def reduce_core(mixture, weight):
    half = mixture.shape[0] // 2
    away = jnp.dot(mixture[half:], weight, preferred_element_type=jnp.float32)
    arrived = exchanged(away.astype(jnp.bfloat16), CORE)
    own = jnp.dot(mixture[:half], weight, preferred_element_type=jnp.float32)
    return own + arrived.astype(jnp.float32)


def ring_blocks(ring):
    rows = ring.shape[0] // 4
    sent = ring.astype(jnp.bfloat16)
    return [ring[:rows]] + [sent[k * rows : (k + 1) * rows] for k in range(1, 4)]


def reduce_ring(total, *blocks):
    arrived = {mask: exchanged(blocks[mask // 2 - 1], mask) for mask in RING}
    for mask in RING:
        total = total + arrived[mask].astype(jnp.float32)
    return total


def add_exchanged(total, exchange):
    return total + exchange(total.astype(jnp.bfloat16)).astype(jnp.float32)


def shards(
    document_token_embedding,
    doc_lengths,
    docid_embed,
    docid_targets,
    enc_gain,
    dec_gain,
    w_enc_qkv,
    w_enc_out,
    cross_query_key_value_weight,
    w_cross_out,
    docid_head_weight,
):
    section_index = lax.axis_index("section")
    core = section_index % 2
    ring_y = section_index // 2 % 4
    depth = section_index // PLANE
    group_index = section_index // GROUP
    micro_count, row_count, model_width = document_token_embedding.shape
    doc_count = doc_lengths.shape[1]
    doc_span = row_count // doc_count
    decoder_rows = docid_embed.shape[1]
    docid_span = decoder_rows // doc_count
    block_rows = doc_span // 2
    share = docid_span // 2

    index = jnp.arange(row_count)
    source_block = (core ^ (index // (row_count // 2))) * 4 + (ring_y ^ (index // block_rows % 4))
    order_there = source_block * block_rows + index % block_rows
    doc_there, place_there = order_there // doc_span, order_there % doc_span

    def live_rows(doc, place, lengths):
        owner = doc[:, None] == jnp.arange(doc_count)
        return place < jnp.sum(jnp.where(owner, lengths[None, :], 0), axis=1)

    maps_other = exchanged(w_enc_qkv, CORE)
    out_other = exchanged(w_enc_out, CORE)
    half = row_count // 2

    own_start = (core * 4 + ring_y) * block_rows

    def own_of(m):
        start = (jnp.int32(m), own_start, jnp.int32(0))
        return lax.dynamic_slice(
            document_token_embedding, start, (1, block_rows, model_width)
        )[0]

    def spread(finished):
        own = norm_rows(finished, enc_gain[GROUPS]).astype(jnp.bfloat16)
        arrived = [along_z(own, ((7, to), (6, 5 - to))) for to in range(3)]
        for to in range(3):
            own = jnp.where((depth == to) | (depth == 5 - to), arrived[to], own)
        return own

    own_half, away_half = first_terms(
        jnp.stack([core, ring_y]).astype(jnp.int32),
        doc_lengths,
        enc_gain,
        document_token_embedding,
        w_enc_qkv,
        w_enc_out,
    )
    blocks = ring_blocks(own_half + exchanged(away_half, CORE).astype(jnp.float32))
    blocks, own_start, gain_index = lax.optimization_barrier((blocks, own_start, group_index))
    layer_gain = lax.dynamic_index_in_dim(enc_gain, gain_index, 0, keepdims=False)
    current = own_of(0)
    last = micro_count + GROUPS - 2
    onward = [(s, s + GROUP) for s in range(SIZE - GROUP)]
    memories = []
    for step in range(last + 1):
        if step:
            slot = jnp.clip(step - group_index, 0, micro_count - 1)
            lengths = lax.dynamic_index_in_dim(doc_lengths, slot, 0, keepdims=False)
            pieces = ring_pieces(norm_rows(current, layer_gain).astype(jnp.bfloat16))
            if step == last:
                pieces, finished = lax.optimization_barrier((pieces, result_of_first))
                memories.append(spread(finished))
            doc, place = doc_there[:half], place_there[:half]
            allowed = (doc[:, None] == doc[None, :]) & live_rows(doc, place, lengths)[None, :]
            blocks = layer_terms(pieces, allowed, w_enc_qkv, maps_other, w_enc_out, out_other)
            if step == last:
                blocks, memories[-1] = lax.optimization_barrier((blocks, memories[-1]))
        summed = add_exchanged(reduce_ring(*blocks), lambda block: exchanged(block, PLANE))
        result = (current.astype(jnp.float32) + summed).astype(jnp.bfloat16)
        if step == last - 1:
            result_of_first = result
        if step == last:
            memories.append(spread(result))
        if step < last:
            current = lax.ppermute(result, "section", onward)
            if step + 1 < micro_count:
                current = jnp.where(group_index == 0, own_of(step + 1), current)
    memories = [gather_rows(rows) for rows in memories]

    index = jnp.arange(decoder_rows)
    query_doc = ring_y ^ (index // share % doc_count)
    query_place = (core ^ (index // (decoder_rows // 2))) * share + index % share
    query_order = query_doc * docid_span + query_place
    cross_same = query_doc[:, None] == doc_there[None, :]
    dec_normed = norm_rows(docid_embed, dec_gain[0]).astype(jnp.bfloat16)
    own_queries = jnp.dot(
        dec_normed.reshape(-1, model_width),
        cross_query_key_value_weight[0].T,
        preferred_element_type=jnp.float32,
    ).astype(jnp.bfloat16)
    own_queries = own_queries.reshape(micro_count, decoder_rows, -1, HD)

    mixtures = []
    for m in range(micro_count):
        heads = jnp.einsum(
            "rd,qcd->qrc",
            memories[m],
            cross_query_key_value_weight[1:],
            preferred_element_type=jnp.float32,
        ).astype(jnp.bfloat16)
        heads = heads.reshape(2, row_count, -1, HD)
        allowed = cross_same & live_rows(doc_there, place_there, doc_lengths[m])[None, :]
        queries = jnp.take(own_queries[m], query_order, axis=0)
        mixed = attend(queries, heads[0], heads[1], allowed)
        mixtures.append(mixed.reshape(decoder_rows // share, share, -1))
    cross_mixture = jnp.stack(mixtures, 1).reshape(micro_count * decoder_rows, -1)
    cross_sum = reduce_ring(*ring_blocks(reduce_core(cross_mixture, w_cross_out)))
    for partner in ((1, 0, 3, 2, 5, 4, 7, 6), (7, 2, 1, 4, 3, 6, 5, 0), (3, 6, 5, 0, 7, 2, 1, 4)):
        route = tuple(enumerate(partner))
        cross_sum = add_exchanged(cross_sum, lambda block, route=route: along_z(block, route))
    own_docid = lax.dynamic_slice_in_dim(
        docid_embed, ring_y * docid_span + core * share, share, 1
    ).reshape(micro_count * share, model_width)
    closing_own = norm_rows(own_docid.astype(jnp.float32) + cross_sum, dec_gain[1]).astype(
        jnp.bfloat16
    )
    closing = gather_rows(closing_own)

    scores_here = jnp.dot(closing, docid_head_weight, preferred_element_type=jnp.float32)
    vocab_local = docid_head_weight.shape[1]
    index = jnp.arange(micro_count * decoder_rows)
    micro, doc = index // decoder_rows, index // docid_span % doc_count
    half, row = index // share % 2, index % share
    source = (((half ^ core) * doc_count + (doc ^ ring_y)) * micro_count + micro) * share + row
    scores_vocab = jnp.take(scores_here, source, axis=0).reshape(
        micro_count, decoder_rows, vocab_local
    )
    vocab_start = section_index * vocab_local
    matches = docid_targets[..., None] == vocab_start + jnp.arange(vocab_local)
    sums = jnp.stack(
        [
            jnp.sum(jnp.exp(scores_vocab), axis=-1),
            jnp.sum(jnp.where(matches, scores_vocab, 0.0), axis=-1),
        ]
    ).reshape(1, -1)
    axes = ("section", "rep")
    planes = lax.axis_size("rep")
    size = SIZE * planes
    everything = lax.all_to_all(
        jnp.broadcast_to(sums[None], (size, *sums.shape)), axes, 0, 0, tiled=True
    )
    sums = jnp.sum(everything.reshape(SIZE, planes, -1), axis=0)
    exponent_total, picked = jnp.moveaxis(sums.reshape(planes, 2, -1), 1, 0)
    token_losses = jnp.log(exponent_total) - picked
    token_loss = lax.dynamic_index_in_dim(
        token_losses, lax.axis_index("rep"), 0, keepdims=False
    ).reshape(micro_count, decoder_rows)
    mean_loss = jnp.mean(token_losses)
    return (scores_vocab.astype(jnp.bfloat16), token_loss, mean_loss)


def solution(mesh):
    in_specs = (
        P("rep", None, None),
        P("rep", None),
        P("rep", None, None),
        P("rep", None),
        P(),
        P(),
        P(None, "section", None),
        P("section", None),
        P(None, "section", None),
        P("section", None),
        P(None, "section"),
    )
    out_specs = (P("rep", None, "section"), P("rep", None), P())
    return jax.shard_map(shards, mesh=mesh, in_specs=in_specs, out_specs=out_specs, check_vma=False)
```
